32 devices in a mesh: dp: 8 (over z, x), head: 4 (over y, core).
Axes of the slice: x: 2, y: 2, z: 4, core: 2. Of those that a mesh axis runs over, the one named last changes fastest.
Arguments:
- tokens: bfloat16 [32768, 768], P(('dp', 'head')), may hold values from -6 to 6
- cotangent: bfloat16 [32768, 768], P(('dp', 'head')), may hold values from -6 to 6
- w_qkv: bfloat16 [768, 12, 192], P(None, 'head'), may hold values from -0.21875 to 0.21875
- bias_qv: bfloat16 [12, 2, 64], P('head'), may hold values from -3 to 3
- w_out: bfloat16 [12, 64, 768], P('head'), may hold values from -1.25 to 1.25
- bias_out: float32 [768], replicated, may hold values from -3 to 3
- gain_one: float32 [768], replicated, may hold values from 0.5 to 1.5
- beta_one: float32 [768], replicated, may hold values from -3 to 3
- w_up: bfloat16 [768, 3072], replicated, may hold values from -0.21875 to 0.21875
- bias_up: float32 [3072], replicated, may hold values from -3 to 3
- w_down: bfloat16 [3072, 768], replicated, may hold values from -0.109375 to 0.109375
- bias_down: float32 [768], replicated, may hold values from -3 to 3
- gain_two: float32 [768], replicated, may hold values from 0.5 to 1.5
- beta_two: float32 [768], replicated, may hold values from -3 to 3
Outputs:
- layer_out: bfloat16 [32768, 768], P(('dp', 'head'))
- input_grad: float32 [32768, 768], P(('dp', 'head'))
- grad_qkv: float32 [768, 12, 192], P('dp', 'head')
- grad_bias_qv: float32 [12, 2, 64], P('head', None, 'dp')
- grad_out: float32 [12, 64, 768], P('head', None, 'dp')
- grad_bias_out: float32 [768], replicated
- grad_gain_one: float32 [768], replicated
- grad_beta_one: float32 [768], replicated
- grad_w_up: float32 [768, 3072], replicated
- grad_bias_up: float32 [3072], replicated
- grad_w_down: float32 [3072, 768], replicated
- grad_bias_down: float32 [768], replicated
- grad_gain_two: float32 [768], replicated
- grad_beta_two: float32 [768], replicated
The draws below stay inside these ranges and needn't reach their ends.
All inputs are finite; a program needn't handle non-finite values.
Results may differ from the reference program's by a relative error of at most 0.017.
Values may be sent and summed in bfloat16 or wider, within the bound.
No kernel may reach another device: no remote copies, remote signals or barrier semaphores. Data moves between devices by JAX's collectives and lax.ppermute only.
A program may use at most 192 MiB of HBM per device.

```python
import math
import jax
import jax.numpy as jnp
from jax import lax

D = 768
HEADS = 12
HD = 64
FF = 3072
SEQ = 128
TOKENS = 32768


def levels(own_key, shape, shards, low, high):
    gain, own = 1.0, jax.random.fold_in(own_key, 6)
    for axis_at, blocks in shards:
        steps = jnp.exp(jax.random.uniform(jax.random.fold_in(own, axis_at), (blocks,), jnp.float32, low / len(shards), high / len(shards)))
        gain = gain * jnp.repeat(steps, shape[axis_at] // blocks).reshape([-1 if axis == axis_at else 1 for axis in range(len(shape))])
    return gain


def normal_values(stream_key, dims, spread, bound, cuts=(), kind=jnp.bfloat16):
    entries = jax.random.normal(stream_key, dims, jnp.float32) * spread
    if len(cuts) > 0:
        entries = levels(stream_key, dims, cuts, -0.22, 0.18) * entries
    return jnp.clip(entries, min=-bound, max=bound).astype(kind)


def setup_inputs(seed: int = 0) -> dict:
    streams_of = jax.random.split(jax.random.key(seed), 15)
    return {
        "tokens": normal_values(streams_of[0], (TOKENS, D), 1.0, 6.0, ((0, 32),)),
        "cotangent": normal_values(streams_of[1], (TOKENS, D), 1.0, 6.0, ((0, 32),)),
        "w_qkv": normal_values(streams_of[2], (D, HEADS, 3 * HD), D ** -0.5, 0.21875, ((1, 4),)),
        "bias_qv": normal_values(streams_of[3], (HEADS, 2, HD), 0.5, 3.0, ((0, 4),)),
        "w_out": normal_values(streams_of[4], (HEADS, HD, D), (D // 32) ** -0.5, 1.25, ((0, 4),)),
        "bias_out": normal_values(streams_of[5], (D,), 0.5, 3.0, (), jnp.float32),
        "gain_one": jnp.clip(1.0 + 0.1 * jax.random.normal(streams_of[6], (D,), jnp.float32), 0.5, 1.5),
        "beta_one": normal_values(streams_of[7], (D,), 0.5, 3.0, (), jnp.float32),
        "w_up": normal_values(streams_of[8], (D, FF), D ** -0.5, 0.21875),
        "bias_up": normal_values(streams_of[9], (FF,), 0.5, 3.0, (), jnp.float32),
        "w_down": normal_values(streams_of[10], (FF, D), FF ** -0.5, 0.109375),
        "bias_down": normal_values(streams_of[11], (D,), 0.5, 3.0, (), jnp.float32),
        "gain_two": jnp.clip(1.0 + 0.1 * jax.random.normal(streams_of[12], (D,), jnp.float32), 0.5, 1.5),
        "beta_two": normal_values(streams_of[13], (D,), 0.5, 3.0, (), jnp.float32),
    }


@jax.custom_vjp
def low(v):
    return lax.optimization_barrier(v.astype(jnp.bfloat16)).astype(jnp.float32)

@jax.custom_vjp
def low_back(v):
    return v

def low_keep(v):
    return (low(v), None)

def low_pass(kept, grad):
    return (grad,)

def back_keep(v):
    return (v, None)

def back_low(kept, grad):
    return (low(grad),)
low.defvjp(low_keep, low_pass)
low_back.defvjp(back_keep, back_low)
epsilon = 1e-12
highest = lax.Precision.HIGHEST

def layer_norm(values, norm_gain, norm_shift):
    center = values - lax.optimization_barrier(jnp.mean(values, axis=-1, keepdims=True))
    variance = lax.optimization_barrier(jnp.mean(center * center, axis=-1, keepdims=True))
    return center * lax.rsqrt(variance + epsilon) * norm_gain + norm_shift

def layer(params, inputs):
    w_qkv, bias_qv, w_out, bias_out, gain_one, beta_one, w_up, bias_up, w_down, bias_down, gain_two, beta_two = params
    length = inputs.shape[0]
    raw_qkv = jnp.dot(inputs, w_qkv.reshape(D, HEADS * 3 * HD), precision=highest)
    raw_qkv = raw_qkv.reshape(length, HEADS, 3, HD)
    full_bias = jnp.stack([bias_qv[:, 0], jnp.zeros_like(bias_qv[:, 0]), bias_qv[:, 1]], axis=1)
    projected = low_back(low(raw_qkv + full_bias)).reshape(length // SEQ, SEQ, HEADS, 3, HD)
    queries = projected[:, :, :, 0]
    keyed = projected[:, :, :, 1]
    valued = projected[:, :, :, 2]
    scores = low_back(jnp.einsum('bqhd,bkhd->bhqk', queries, keyed, precision=highest) * HD ** (-0.5))
    attn_probs = jax.nn.softmax(scores, axis=-1)
    context = jnp.einsum('bhqk,bkhd->bqhd', low(attn_probs), valued, precision=highest)
    context = low_back(low(context)).reshape(length, D)
    attention = low_back(jnp.dot(context, w_out.reshape(D, D), precision=highest) + bias_out)
    normed_one = layer_norm(inputs + attention, gain_one, beta_one)
    hidden_pre = low_back(jnp.dot(low(normed_one), w_up, precision=highest) + bias_up)
    activated = low(jax.nn.gelu(hidden_pre, approximate=False))
    ffn_out = low_back(jnp.dot(activated, w_down, precision=highest) + bias_down)
    return layer_norm(normed_one + ffn_out, gain_two, beta_two)

def reference(tokens, cotangent, w_qkv, bias_qv, w_out, bias_out, gain_one, beta_one, w_up, bias_up, w_down, bias_down, gain_two, beta_two):
    params = tuple((array.astype(jnp.float32) for array in (w_qkv, bias_qv, w_out, bias_out, gain_one, beta_one, w_up, bias_up, w_down, bias_down, gain_two, beta_two)))
    overall = tokens.shape[0]
    stretch = math.gcd(overall, 4096)
    blocks = overall // stretch
    inputs_all = tokens.astype(jnp.float32).reshape(blocks, stretch, D)
    upstream_all = cotangent.astype(jnp.float32).reshape(blocks, stretch, D)

    def advance(carried, paired):
        inputs, upstream = paired
        result, puller = jax.vjp(layer, params, inputs)
        grad_params, grad_inputs = puller(upstream)
        carried = jax.tree.map(jnp.add, carried, grad_params)
        return (carried, (result.astype(jnp.bfloat16), grad_inputs))
    starting = jax.tree.map(jnp.zeros_like, params)
    summed, (results, grad_inputs) = lax.scan(advance, starting, (inputs_all, upstream_all))
    return (results.reshape(overall, D), grad_inputs.reshape(overall, D), summed[0], summed[1], summed[2], summed[3], summed[4], summed[5], summed[6], summed[7], summed[8], summed[9], summed[10], summed[11])
```

```python
import functools
import math

import jax
import jax.numpy as jnp
from jax import lax
from jax.sharding import PartitionSpec as P

SEQ = 128


epsilon = 1e-12


def matmul_rows(left, right):
    return lax.dot_general(
        left, right, (((0,), (0,)), ((), ())), preferred_element_type=jnp.float32
    )


def matmul_back(left, right):
    return lax.dot_general(
        left, right, (((1,), (1,)), ((), ())), preferred_element_type=jnp.float32
    )


def gelu_exact(values):
    return jax.nn.gelu(values, approximate=False)


def normalize(values, norm_gain, norm_shift):
    center = values - jnp.mean(values, axis=-1, keepdims=True)
    variance = jnp.mean(center * center, axis=-1, keepdims=True)
    inverse = lax.rsqrt(variance + epsilon)
    normal_rows = center * inverse
    return (normal_rows * norm_gain + norm_shift, normal_rows, inverse)


def normalize_back(upstream, normal_rows, inverse, norm_gain):
    grad_unit = upstream * norm_gain
    grad_rows = inverse * (
        grad_unit
        - jnp.mean(grad_unit, axis=-1, keepdims=True)
        - normal_rows * jnp.mean(grad_unit * normal_rows, axis=-1, keepdims=True)
    )
    return (grad_rows, jnp.sum(upstream * normal_rows, axis=0), jnp.sum(upstream, axis=0))


def split_blocks(projected, head_count, seq_length):
    sequences = projected.shape[0] // seq_length
    per_block = math.gcd(sequences, max(1, 512 // seq_length))
    return projected.reshape(sequences // per_block, per_block, seq_length, head_count, 3, -1)


def score_block(queries, keyed):
    factor = float(queries.shape[-1]) ** (-0.5)
    return (
        jnp.einsum("bqhd,bkhd->bhqk", queries, keyed, preferred_element_type=jnp.float32) * factor
    )


def attend_block(section):
    queries = section[:, :, :, 0]
    keyed = section[:, :, :, 1]
    valued = section[:, :, :, 2]
    scores = score_block(queries, keyed)
    highest = jnp.max(scores, axis=-1, keepdims=True)
    exponent = jnp.exp(scores - highest)
    row_total = jnp.sum(exponent, axis=-1, keepdims=True)
    attn_probs = exponent / row_total
    context = jnp.einsum(
        "bhqk,bkhd->bqhd",
        attn_probs.astype(jnp.bfloat16),
        valued,
        preferred_element_type=jnp.float32,
    )
    return (context.astype(jnp.bfloat16), highest + jnp.log(row_total))


def attend_back(pieces):
    section, log_total, grad_context = pieces
    queries = section[:, :, :, 0]
    keyed = section[:, :, :, 1]
    valued = section[:, :, :, 2]
    factor = float(queries.shape[-1]) ** (-0.5)
    attn_probs = jnp.exp(score_block(queries, keyed) - log_total)
    grad_probs = jnp.einsum(
        "bqhd,bkhd->bhqk", grad_context, valued, preferred_element_type=jnp.float32
    )
    inner = jnp.sum(grad_probs * attn_probs, axis=-1, keepdims=True)
    grad_scores = (attn_probs * (grad_probs - inner)).astype(jnp.bfloat16)
    grad_values = jnp.einsum(
        "bhqk,bqhd->bkhd",
        attn_probs.astype(jnp.bfloat16),
        grad_context,
        preferred_element_type=jnp.float32,
    )
    grad_queries = (
        jnp.einsum("bhqk,bkhd->bqhd", grad_scores, keyed, preferred_element_type=jnp.float32)
        * factor
    )
    grad_keyed = (
        jnp.einsum("bhqk,bqhd->bkhd", grad_scores, queries, preferred_element_type=jnp.float32)
        * factor
    )
    return jnp.stack([grad_queries, grad_keyed, grad_values], axis=-2).astype(jnp.bfloat16)


def attention_forward(projected, head_count, seq_length):
    sections = split_blocks(projected, head_count, seq_length)
    context, log_total = lax.map(attend_block, sections)
    return (context.reshape(projected.shape[0], -1), log_total)


def attention_backward(projected, log_total, grad_context, head_count, seq_length):
    sections = split_blocks(projected, head_count, seq_length)
    grad_shaped = grad_context.reshape(sections.shape[:4] + (-1,))
    grads = lax.map(attend_back, (sections, log_total, grad_shaped))
    return grads.reshape(projected.shape[0], -1)


AXES = ("dp", "head")


class Net:
    def __init__(self, dp_size, head_size):
        self.size = dp_size * head_size
        self.index = lax.axis_index("dp") * head_size + lax.axis_index("head")
        self.head_bits = [1 << k for k in range(head_size.bit_length() - 1)]
        self.dp_bits = [head_size << k for k in range(dp_size.bit_length() - 1)]

    def bit(self, mask):
        return (self.index // mask) % 2

    def swap(self, values, mask):
        return lax.ppermute(values, AXES, [(i, i ^ mask) for i in range(self.size)])


def half(values, which, axis):
    part = values.shape[axis] // 2
    return lax.dynamic_slice_in_dim(values, which * part, part, axis)


def reduce_half(net, values, mask, axis):
    own = net.bit(mask)
    received = net.swap(half(values, 1 - own, axis), mask)
    kept = half(values, own, axis)
    return (kept.astype(jnp.float32) + received.astype(jnp.float32)).astype(jnp.bfloat16)


def join_half(net, values, mask, axis):
    own = net.bit(mask)
    received = net.swap(values, mask)
    return jnp.where(
        own == 0,
        jnp.concatenate([values, received], axis),
        jnp.concatenate([received, values], axis),
    )


def routes(net):
    first, second = net.dp_bits[0], net.head_bits[-1]
    rest = net.head_bits[1:-1] + net.dp_bits[1:]
    return net.head_bits[0], (first, second), (second, first), rest


def reduce_square(net, squares):
    core, *orders, rest = routes(net)
    mine = reduce_half(net, squares, core, 0)
    done = []
    for color, order in enumerate(orders):
        part = mine[color]
        for mask in order:
            part = reduce_half(net, part, mask, 0)
        done.append(part)
    done = jnp.stack(done)
    for mask in rest:
        done = reduce_half(net, done, mask, 1)
    return done


def gather_square(net, done):
    core, *orders, rest = routes(net)
    for mask in reversed(rest):
        done = join_half(net, done, mask, 1)
    parts = []
    for color, order in enumerate(orders):
        part = done[color]
        for mask in reversed(order):
            part = join_half(net, part, mask, 0)
        parts.append(part)
    return join_half(net, jnp.stack(parts), core, 0)


def reduce_heads(net, groups, dp_size):
    for mask in net.head_bits:
        half_count = groups.shape[0] // 2
        pairs = groups.reshape((half_count, 2) + groups.shape[1:])
        received = net.swap(pairs[:, 1], mask)
        groups = (pairs[:, 0].astype(jnp.float32) + received.astype(jnp.float32)).astype(jnp.bfloat16)
    rows = groups[0].reshape((dp_size, -1) + groups.shape[2:])
    for mask in net.dp_bits:
        count = rows.shape[0] // 2
        own = net.bit(mask)
        pairs = rows.reshape((count, 2) + rows.shape[1:])
        received = net.swap(lax.dynamic_index_in_dim(pairs, 1 - own, 1, False), mask)
        kept = lax.dynamic_index_in_dim(pairs, own, 1, False)
        rows = (kept.astype(jnp.float32) + received.astype(jnp.float32)).astype(jnp.bfloat16)
    return rows[0]


def sum_everywhere(net, values):
    for mask in net.head_bits + net.dp_bits:
        values = values + net.swap(values, mask)
    return values


def gather_heads(net, values):
    parts = values[None]
    for mask in net.head_bits:
        parts = jnp.concatenate([parts, net.swap(parts, mask)], 0)
    return parts


def shards(
    dp_size,
    head_size,
    tokens,
    cotangent,
    w_qkv,
    bias_qv,
    w_out,
    bias_out,
    gain_one,
    beta_one,
    w_up,
    bias_up,
    w_down,
    bias_down,
    gain_two,
    beta_two,
):
    net = Net(dp_size, head_size)
    model_width = tokens.shape[1]
    local_heads = w_qkv.shape[1]
    heads = local_heads * head_size
    head_dim = w_qkv.shape[2] // 3
    w_qkv = gather_heads(net, w_qkv.reshape(model_width, -1))
    bias_qv = gather_heads(net, bias_qv)
    w_out = gather_heads(net, w_out.reshape(-1, model_width))
    bias_wide = bias_qv.astype(jnp.float32)
    full_bias = jnp.stack(
        [bias_wide[:, :, 0], jnp.zeros_like(bias_wide[:, :, 0]), bias_wide[:, :, 1]], axis=2
    ).reshape(-1)
    flat_qkv = jnp.swapaxes(w_qkv, 0, 1).reshape(model_width, -1)
    out_rows = w_out.reshape(-1, model_width)
    projected = (
        jnp.dot(tokens, flat_qkv, preferred_element_type=jnp.float32) + full_bias
    ).astype(jnp.bfloat16)
    context, log_total = attention_forward(projected, heads, SEQ)
    attention = jnp.dot(context, out_rows, preferred_element_type=jnp.float32) + bias_out
    normed_one, unit_one, scale_one = normalize(
        tokens.astype(jnp.float32) + attention, gain_one, beta_one
    )
    normed_low = normed_one.astype(jnp.bfloat16)
    hidden_pre = jnp.dot(normed_low, w_up, preferred_element_type=jnp.float32) + bias_up
    gelu_value, gelu_pull = jax.vjp(gelu_exact, hidden_pre)
    activated = gelu_value.astype(jnp.bfloat16)
    ffn_out = jnp.dot(activated, w_down, preferred_element_type=jnp.float32) + bias_down
    result, unit_two, scale_two = normalize(normed_one + ffn_out, gain_two, beta_two)
    layer_out = result.astype(jnp.bfloat16)
    upstream = cotangent.astype(jnp.float32)
    grad_two, grad_gain_two, grad_beta_two = normalize_back(upstream, unit_two, scale_two, gain_two)
    grad_ffn = grad_two.astype(jnp.bfloat16)
    grad_bias_down = jnp.sum(grad_ffn, axis=0, dtype=jnp.float32)
    grad_w_down = matmul_rows(activated, grad_ffn).astype(jnp.bfloat16)
    down_part = reduce_square(net, grad_w_down.reshape(4, -1, model_width))
    grad_active = matmul_back(grad_ffn, w_down)
    grad_pre = gelu_pull(grad_active)[0].astype(jnp.bfloat16)
    grad_bias_up = jnp.sum(grad_pre, axis=0, dtype=jnp.float32)
    quarter = grad_pre.shape[1] // 4
    grad_w_up = jnp.stack(
        [
            matmul_rows(normed_low, grad_pre[:, k * quarter : (k + 1) * quarter]).astype(jnp.bfloat16)
            for k in range(4)
        ]
    )
    up_part = reduce_square(net, grad_w_up)
    grad_normed = grad_two + matmul_back(grad_pre, w_up)
    grad_one, grad_gain_one, grad_beta_one = normalize_back(
        grad_normed, unit_one, scale_one, gain_one
    )
    grad_attention = grad_one.astype(jnp.bfloat16)
    grad_bias_out = jnp.sum(grad_attention, axis=0, dtype=jnp.float32)
    grad_context = matmul_back(grad_attention, out_rows).astype(jnp.bfloat16)
    grad_projected = attention_backward(projected, log_total, grad_context, heads, SEQ)
    input_grad = grad_one + matmul_back(grad_projected, flat_qkv)
    wide = 3 * local_heads * head_dim
    deep = local_heads * head_dim
    groups = jnp.stack(
        [
            jnp.concatenate(
                [
                    matmul_rows(tokens, grad_projected[:, k * wide : (k + 1) * wide]),
                    matmul_rows(grad_attention, context[:, k * deep : (k + 1) * deep]),
                ],
                axis=1,
            ).astype(jnp.bfloat16)
            for k in range(head_size)
        ]
    )
    attn_part = reduce_heads(net, groups, dp_size).astype(jnp.float32)
    rows = attn_part.shape[0]
    grad_qkv = attn_part[:, :wide].reshape(rows, local_heads, 3 * head_dim)
    grad_out = attn_part[:, wide:].T.reshape(local_heads, head_dim, rows)
    sums = jnp.sum(grad_projected, axis=0, dtype=jnp.float32).reshape(
        head_size, local_heads, 3, head_dim
    )
    pair = jnp.stack([sums[:, :, 0], sums[:, :, 2]], axis=2)
    head_index = lax.axis_index("head")
    pair = jnp.stack(
        [lax.dynamic_index_in_dim(pair, head_index ^ k, 0, False) for k in range(head_size)]
    )
    small = (
        grad_bias_out,
        grad_gain_one,
        grad_beta_one,
        grad_bias_up,
        grad_bias_down,
        grad_gain_two,
        grad_beta_two,
        pair.reshape(-1),
    )
    total = sum_everywhere(net, jnp.concatenate(small).reshape(-1, 128)).reshape(-1)
    split = []
    at = 0
    for part in small:
        split.append(total[at : at + part.size])
        at += part.size
    pair = lax.dynamic_index_in_dim(split[7].reshape(pair.shape), head_index, 0, False)
    cut = head_dim // dp_size
    grad_bias_qv = lax.dynamic_slice_in_dim(pair, lax.axis_index("dp") * cut, cut, 2)
    full_down = gather_square(net, down_part).reshape(w_down.shape).astype(jnp.float32)
    full_up = jnp.swapaxes(gather_square(net, up_part), 0, 1).reshape(w_up.shape).astype(jnp.float32)
    return (
        layer_out,
        input_grad,
        grad_qkv,
        grad_bias_qv,
        grad_out,
        split[0],
        split[1],
        split[2],
        full_up,
        split[3],
        full_down,
        split[4],
        split[5],
        split[6],
    )


def solution(mesh):
    return jax.shard_map(
        functools.partial(shards, mesh.shape["dp"], mesh.shape["head"]),
        mesh=mesh,
        in_specs=(
            P(("dp", "head"), None),
            P(("dp", "head"), None),
            P(None, "head", None),
            P("head", None, None),
            P("head", None, None),
            P(),
            P(),
            P(),
            P(),
            P(),
            P(),
            P(),
            P(),
            P(),
        ),
        out_specs=(
            P(("dp", "head"), None),
            P(("dp", "head"), None),
            P("dp", "head", None),
            P("head", None, "dp"),
            P("head", None, "dp"),
            P(),
            P(),
            P(),
            P(),
            P(),
            P(),
            P(),
            P(),
            P(),
        ),
        check_vma=False,
    )
```

```python
import functools
import math

import jax
import jax.numpy as jnp
from jax import lax
from jax.experimental import pallas as pl
from jax.experimental.pallas import tpu as pltpu
from jax.sharding import PartitionSpec as P

SEQ = 128
AXES = ("dp", "head")
f32 = jnp.float32
bf16 = jnp.bfloat16
epsilon = 1e-12
ROOM = 58

def dot(left, right, dims=(1, 0)):
    return lax.dot_general(
        left, right, (((dims[0],), (dims[1],)), ((), ())), preferred_element_type=f32
    )


def params(mib):
    return pltpu.CompilerParams(vmem_limit_bytes=mib * 1024 * 1024)


def cost(macs, moved, exps=0):
    return pl.CostEstimate(flops=1, bytes_accessed=1, transcendentals=0)


def whole(*shape):
    return pl.BlockSpec(shape, lambda *_: (0,) * len(shape))


def shape_of(kind, *shape):
    return jax.ShapeDtypeStruct(shape, kind)


def column_sums(values):
    return jnp.sum(values, axis=0, keepdims=True)


def attend_kernel(heads, head_dim, parts, tokens_ref, *refs):
    weight_refs = refs[:parts]
    projected_ref, context_ref, probs_ref = refs[parts:]
    factor = float(head_dim) ** -0.5
    tile = tokens_ref.shape[0]
    wide = projected_ref.shape[2]
    for group, weight_ref in enumerate(weight_refs):
        bias = weight_ref[wide : wide + 1, :wide].astype(f32)
        projected_ref[group] = (
            dot(tokens_ref[...], weight_ref[:wide], (1, 1)) + bias
        ).astype(bf16)
    pairs = [(start, head) for start in range(0, tile, SEQ) for head in range(heads)]
    for group in range(parts):

        def part(start, head, k):
            at = (3 * head + k) * head_dim
            return projected_ref[group, start : start + SEQ, at : at + head_dim]

        scores = [dot(part(s, h, 0), part(s, h, 1), (1, 1)) * factor for s, h in pairs]
        tops = [jnp.max(x, axis=1, keepdims=True) for x in scores]
        exps = [jnp.exp(x - t) for x, t in zip(scores, tops)]
        sums = [jnp.sum(x, axis=1, keepdims=True) for x in exps]
        probs = [(x * (1.0 / t)).astype(bf16) for x, t in zip(exps, sums)]
        for (s, h), p in zip(pairs, probs):
            probs_ref[group * heads + h, s : s + SEQ] = p
        outs = [dot(p, part(s, h, 2)) for (s, h), p in zip(pairs, probs)]
        for k, start in enumerate(range(0, tile, SEQ)):
            context_ref[group, start : start + SEQ] = jnp.concatenate(
                outs[k * heads : (k + 1) * heads], axis=1
            ).astype(bf16)


def attend(tokens, weights, heads, tile=256):
    wide = weights[0].shape[0] - 16
    groups = len(weights)
    rows, width = tokens.shape
    head_dim = wide // (3 * heads)

    def by_group(count, columns):
        return pl.BlockSpec((count, tile, columns), lambda i: (0, i, 0))

    return pl.pallas_call(
        functools.partial(attend_kernel, heads, head_dim, groups),
        grid=(rows // tile,),
        in_specs=[pl.BlockSpec((tile, width), lambda i: (i, 0))] + [whole(wide + 16, width)] * groups,
        out_specs=[
            by_group(groups, wide),
            by_group(groups, wide // 3),
            by_group(groups * heads, SEQ),
        ],
        out_shape=[
            shape_of(bf16, groups, rows, wide),
            shape_of(bf16, groups, rows, wide // 3),
            shape_of(bf16, groups * heads, rows, SEQ),
        ],
        compiler_params=params(ROOM),
        cost_estimate=cost(groups * rows * wide * (width + 4 * SEQ), 4 * groups * rows * wide),
        name="attend",
    )(tokens, *weights)


def normal(values):
    center = values - jnp.mean(values, axis=1, keepdims=True)
    inverse = lax.rsqrt(jnp.mean(center * center, axis=1, keepdims=True) + epsilon)
    return center * inverse, inverse


def normal_back(upstream, unit, inverse, gain):
    grad = upstream * gain
    return inverse * (
        grad
        - jnp.mean(grad, axis=1, keepdims=True)
        - unit * jnp.mean(grad * unit, axis=1, keepdims=True)
    )


def gelu_pair(values):
    decay = jnp.exp(values * values * -0.5)
    turn = 1.0 / (1.0 + (0.3275911 / math.sqrt(2.0)) * jnp.abs(values))
    series = 0.5 * 1.061405429
    for coefficient in (-1.453152027, 1.421413741, -0.284496736, 0.254829592):
        series = 0.5 * coefficient + turn * series
    tail = turn * series * decay
    spread = jnp.where(values >= 0.0, 1.0 - tail, tail)
    return values * spread, spread + values * (decay * (1.0 / math.sqrt(2.0 * math.pi)))


def fetch(sources, targets, semaphores):
    return [
        pltpu.make_async_copy(source, target, semaphores.at[k])
        for k, (source, target) in enumerate(zip(sources, targets))
    ]


def square_copies(w_up_hbm, w_down_hbm, w_up_ref, w_down_ref, semaphores, chunk):
    copies = []
    for square in range(w_down_ref.shape[0] // chunk):
        here = pl.ds(square * chunk, chunk)
        up = pltpu.make_async_copy(
            w_up_hbm.at[:, here], w_up_ref.at[:, here], semaphores.at[0, square]
        )
        down = pltpu.make_async_copy(
            w_down_hbm.at[here], w_down_ref.at[here], semaphores.at[1, square]
        )
        copies.append((up, down))
    return copies


def forward_kernel(chunk, parts, groups, tiles, index_ref, tokens_ref, cot_ref, *refs):
    context_refs, refs = refs[:parts], refs[parts:]
    out_weight_refs, refs = refs[:groups], refs[groups:]
    w_up_hbm, w_down_hbm, vec_ref, bias_up_ref = refs[:4]
    slope_ref, low_ref, unit_ref, scale_ref = refs[4:8]
    out_ref, grad_two_ref, grad_ffn_ref, sums_ref, sent_ref, kept_ref = refs[8:14]
    act_ref, whole_grad_ref, w_up_ref, w_down_ref, semaphores = refs[14:]
    step = pl.program_id(0)
    tile = tokens_ref.shape[0]
    copies = square_copies(w_up_hbm, w_down_hbm, w_up_ref, w_down_ref, semaphores, chunk)

    @pl.when(step == 0)
    def _():
        for pair in copies:
            for copy in pair:
                copy.start()
        sums_ref[...] = jnp.zeros_like(sums_ref)

    @pl.when(step < tiles)
    def _():
        rows = pl.ds(pl.multiple_of(step * tile, tile), tile)
        bias_out, gain_one, beta_one, bias_down, gain_two, beta_two = (
            vec_ref[k : k + 1] for k in range(6)
        )
        attention = bias_out
        shared = groups // parts
        for group, weight_ref in enumerate(out_weight_refs):
            attention = attention + dot(
                context_refs[group // shared][group % shared], weight_ref[...]
            )
        unit_one, scale_one = normal(tokens_ref[...].astype(f32) + attention)
        normed = unit_one * gain_one + beta_one
        low = normed.astype(bf16)
        unit_ref[...] = unit_one
        scale_ref[...] = scale_one
        low_ref[...] = low
        total = normed + bias_down
        for square, pair in enumerate(copies):
            cols = slice(square * chunk, (square + 1) * chunk)

            @pl.when(step == 0)
            def _():
                for copy in pair:
                    copy.wait()

            hidden = dot(low, w_up_ref[:, cols]) + bias_up_ref[:, cols]
            value, slope = gelu_pair(hidden)
            value = value.astype(bf16)
            act_ref[square, rows] = value
            slope_ref[square] = slope.astype(bf16)
            total = total + dot(value, w_down_ref[cols])
        unit_two, scale_two = normal(total)
        out_ref[...] = (unit_two * gain_two + beta_two).astype(bf16)
        upstream = cot_ref[...].astype(f32)
        grad_two = normal_back(upstream, unit_two, scale_two, gain_two)
        grad_two_ref[...] = grad_two
        grad_ffn = grad_two.astype(bf16)
        grad_ffn_ref[...] = grad_ffn
        whole_grad_ref[rows] = grad_ffn
        sums_ref[0:1] += column_sums(upstream * unit_two)
        sums_ref[1:2] += column_sums(upstream)
        sums_ref[2:3] += column_sums(grad_ffn.astype(f32))

    for place, done_ref in enumerate((sent_ref, kept_ref)):

        @pl.when((step >= tiles + 2 * place) & (step < tiles + 2 * place + 2))
        def _():
            square = index_ref[step - tiles]
            first = index_ref[4 + (step - tiles) % 2]
            half = done_ref.shape[1]
            for n in range(2):
                left = act_ref[square, :, n * half : (n + 1) * half]
                done_ref[first ^ n] = dot(left, whole_grad_ref[...], (0, 0)).astype(bf16)


def half_squares(skip, half, width):
    return pl.BlockSpec((2, half, width), lambda i, *_: (jnp.clip(i - skip, 0, 1), 0, 0))


def forward(
    index, tokens, cotangent, contexts, out_weights, w_up, w_down, vectors, bias_up, tile=256
):
    rows, width = tokens.shape
    ff = w_up.shape[1]
    chunk = ff // 4
    deep = contexts[0].shape[2]
    tiles = rows // tile

    def row(n):
        return pl.BlockSpec((tile, n), lambda i, *_: (jnp.minimum(i, tiles - 1), 0))

    def stay(*shape):
        return pl.BlockSpec(shape, lambda *_: (0,) * len(shape), pipeline_mode=pl.Buffered(1))

    anywhere = pl.BlockSpec(memory_space=pl.ANY)
    return pl.pallas_call(
        functools.partial(forward_kernel, chunk, len(contexts), len(out_weights), tiles),
        grid_spec=pltpu.PrefetchScalarGridSpec(
            num_scalar_prefetch=1,
            grid=(tiles + 4,),
            in_specs=[row(width), row(width)]
            + [
                pl.BlockSpec(
                    (c.shape[0], tile, deep), lambda i, *_: (0, jnp.minimum(i, tiles - 1), 0)
                )
                for c in contexts
            ]
            + [stay(*w.shape) for w in out_weights]
            + [anywhere, anywhere, stay(8, width), stay(1, ff)],
            out_specs=[
                pl.BlockSpec((4, tile, chunk), lambda i, *_: (0, jnp.minimum(i, tiles - 1), 0)),
                row(width),
                row(width),
                row(1),
                row(width),
                row(width),
                row(width),
                whole(8, width),
                half_squares(tiles, chunk // 2, width),
                half_squares(tiles + 2, chunk // 2, width),
            ],
            scratch_shapes=[
                pltpu.VMEM((4, rows, chunk), bf16),
                pltpu.VMEM((rows, width), bf16),
                pltpu.VMEM((width, ff), bf16),
                pltpu.VMEM((ff, width), bf16),
                pltpu.SemaphoreType.DMA((2, 4)),
            ],
        ),
        out_shape=[
            shape_of(bf16, 4, rows, chunk),
            shape_of(bf16, rows, width),
            shape_of(f32, rows, width),
            shape_of(f32, rows, 1),
            shape_of(bf16, rows, width),
            shape_of(f32, rows, width),
            shape_of(bf16, rows, width),
            shape_of(f32, 8, width),
            shape_of(bf16, 4, chunk // 2, width),
            shape_of(bf16, 4, chunk // 2, width),
        ],
        compiler_params=params(ROOM),
        cost_estimate=cost(rows * width * (3 * ff + width), 12 * rows * ff, rows * ff),
        name="forward",
    )(index, tokens, cotangent, *contexts, *out_weights, w_up, w_down, vectors, bias_up)


def backward_kernel(
    chunk,
    tiles,
    index_ref,
    grad_ffn_ref,
    slope_ref,
    grad_two_ref,
    low_ref,
    unit_ref,
    scale_ref,
    w_up_hbm,
    w_down_hbm,
    vec_ref,
    grad_one_ref,
    grad_att_ref,
    sums_ref,
    bias_ref,
    sent_ref,
    kept_ref,
    grad_pre_ref,
    turned_ref,
    w_up_ref,
    w_down_ref,
    semaphores,
):
    step = pl.program_id(0)
    tile = grad_ffn_ref.shape[0]
    copies = square_copies(w_up_hbm, w_down_hbm, w_up_ref, w_down_ref, semaphores, chunk)

    @pl.when(step == 0)
    def _():
        for up, down in copies:
            down.start()
            up.start()
        sums_ref[...] = jnp.zeros_like(sums_ref)
        bias_ref[...] = jnp.zeros_like(bias_ref)

    for at in range(tiles):

        @pl.when(step == at)
        def _():
            turned_ref[:, at * tile : (at + 1) * tile] = low_ref[...].T

    @pl.when(step < tiles)
    def _():
        rows = pl.ds(pl.multiple_of(step * tile, tile), tile)
        total = grad_two_ref[...]
        grad_ffn = grad_ffn_ref[...]
        for square, pair in enumerate(copies):
            cols = slice(square * chunk, (square + 1) * chunk)

            @pl.when(step == 0)
            def _():
                for copy in pair:
                    copy.wait()

            grad_pre = dot(grad_ffn, w_down_ref[cols], (1, 1)) * slope_ref[square].astype(f32)
            grad_pre = grad_pre.astype(bf16)
            grad_pre_ref[square, rows] = grad_pre
            bias_ref[:, cols] += column_sums(grad_pre.astype(f32))
            total = total + dot(grad_pre, w_up_ref[:, cols], (1, 1))
        unit = unit_ref[...]
        grad_one = normal_back(total, unit, scale_ref[...], vec_ref[1:2])
        grad_one_ref[...] = grad_one
        grad_att = grad_one.astype(bf16)
        grad_att_ref[...] = grad_att
        sums_ref[0:1] += column_sums(total * unit)
        sums_ref[1:2] += column_sums(total)
        sums_ref[2:3] += column_sums(grad_att.astype(f32))

    for place, done_ref in enumerate((sent_ref, kept_ref)):

        @pl.when((step >= tiles + 2 * place) & (step < tiles + 2 * place + 2))
        def _():
            square = index_ref[step - tiles]
            first = index_ref[4 + (step - tiles) % 2]
            half = done_ref.shape[1]
            for n in range(2):
                left = turned_ref[n * half : (n + 1) * half]
                done_ref[first ^ n] = dot(left, grad_pre_ref[square]).astype(bf16)


def backward(
    index, grad_ffn, slope, grad_two, low, unit, scale, w_up, w_down, vectors, tile=256
):
    rows, width = grad_ffn.shape
    ff = w_up.shape[1]
    chunk = ff // 4
    tiles = rows // tile

    def row(n):
        return pl.BlockSpec((tile, n), lambda i, *_: (jnp.minimum(i, tiles - 1), 0))

    anywhere = pl.BlockSpec(memory_space=pl.ANY)
    return pl.pallas_call(
        functools.partial(backward_kernel, chunk, tiles),
        grid_spec=pltpu.PrefetchScalarGridSpec(
            num_scalar_prefetch=1,
            grid=(tiles + 4,),
            in_specs=[
                row(width),
                pl.BlockSpec((4, tile, chunk), lambda i, *_: (0, jnp.minimum(i, tiles - 1), 0)),
                row(width),
                row(width),
                row(width),
                row(1),
                anywhere,
                anywhere,
                whole(8, width),
            ],
            out_specs=[
                row(width),
                row(width),
                whole(8, width),
                whole(1, ff),
                half_squares(tiles, width // 2, chunk),
                half_squares(tiles + 2, width // 2, chunk),
            ],
            scratch_shapes=[
                pltpu.VMEM((4, rows, chunk), bf16),
                pltpu.VMEM((width, rows), bf16),
                pltpu.VMEM((width, ff), bf16),
                pltpu.VMEM((ff, width), bf16),
                pltpu.SemaphoreType.DMA((2, 4)),
            ],
        ),
        out_shape=[
            shape_of(f32, rows, width),
            shape_of(bf16, rows, width),
            shape_of(f32, 8, width),
            shape_of(f32, 1, ff),
            shape_of(bf16, 4, width // 2, chunk),
            shape_of(bf16, 4, width // 2, chunk),
        ],
        compiler_params=params(ROOM),
        cost_estimate=cost(rows * width * 3 * ff, 10 * rows * ff),
        name="backward",
    )(index, grad_ffn, slope, grad_two, low, unit, scale, w_up, w_down, vectors)


def attend_back_kernel(
    heads, head_dim, parts, groups, tiles, tokens_ref, grad_att_ref, grad_one_ref, *refs
):
    projected_refs, refs = refs[:parts], refs[parts:]
    probs_refs, refs = refs[:parts], refs[parts:]
    context_refs, refs = refs[:parts], refs[parts:]
    weight_refs, refs = refs[:groups], refs[groups:]
    out_weight_refs, refs = refs[:groups], refs[groups:]
    input_ref, sums_ref, sent_ref, kept_ref = refs[:4]
    grad_projected_ref, grad_context_ref, tokens_t, grad_att_t = refs[4:]
    step = pl.program_id(0)
    tile = grad_att_ref.shape[0]
    wide = grad_projected_ref.shape[2]
    factor = float(head_dim) ** -0.5

    @pl.when(step == 0)
    def _():
        sums_ref[...] = jnp.zeros_like(sums_ref)

    for at in range(tiles):

        @pl.when(step == at)
        def _():
            tokens_t[:, at * tile : (at + 1) * tile] = tokens_ref[...].T
            grad_att_t[:, at * tile : (at + 1) * tile] = grad_att_ref[...].T

    @pl.when(step < tiles)
    def _():
        begin = step * tile
        places = [(k, g) for k in range(parts) for g in range(groups // parts)]
        for group, (k, g) in enumerate(places):
            grad_context_ref[group] = dot(
                grad_att_ref[...], out_weight_refs[group][...], (1, 1)
            ).astype(bf16)
        pairs = [(start, head) for start in range(0, tile, SEQ) for head in range(heads)]
        for group, (k, g) in enumerate(places):

            def part(start, head, which):
                at = (3 * head + which) * head_dim
                return projected_refs[k][g, start : start + SEQ, at : at + head_dim]

            def up(start, head):
                return grad_context_ref[
                    group, start : start + SEQ, head * head_dim : (head + 1) * head_dim
                ]

            def low(start, head):
                return probs_refs[k][g * heads + head, start : start + SEQ]

            grad_probs = [dot(up(s, h), part(s, h, 2), (1, 1)) for s, h in pairs]
            inner = [
                jnp.sum(x * low(s, h).astype(f32), axis=1, keepdims=True)
                for x, (s, h) in zip(grad_probs, pairs)
            ]
            grad_scores = [
                (low(s, h).astype(f32) * (x - i)).astype(bf16)
                for x, i, (s, h) in zip(grad_probs, inner, pairs)
            ]
            grad_v = [dot(low(s, h), up(s, h), (0, 0)) for s, h in pairs]
            grad_q = [dot(x, part(s, h, 1)) * factor for x, (s, h) in zip(grad_scores, pairs)]
            grad_k = [
                dot(x, part(s, h, 0), (0, 0)) * factor for x, (s, h) in zip(grad_scores, pairs)
            ]
            for n, start in enumerate(range(0, tile, SEQ)):
                pieces = [
                    x
                    for j in range(n * heads, (n + 1) * heads)
                    for x in (grad_q[j], grad_k[j], grad_v[j])
                ]
                at = pl.ds(pl.multiple_of(begin + start, SEQ), SEQ)
                grad_projected_ref[group, at] = jnp.concatenate(pieces, axis=1).astype(bf16)
        total = grad_one_ref[...]
        rows = pl.ds(pl.multiple_of(begin, tile), tile)
        for group, (k, g) in enumerate(places):
            grad_projected = grad_projected_ref[group, rows]
            sums_ref[group : group + 1] += column_sums(grad_projected.astype(f32))
            total = total + dot(grad_projected, weight_refs[group][:wide])
        input_ref[...] = total

    for place, done_ref in enumerate((sent_ref, kept_ref)):
        for at in range(parts):

            @pl.when(step == tiles + parts * place + at)
            def _():
                group = 2 * at + 1 - place
                done_ref[0, :, :wide] = dot(tokens_t[...], grad_projected_ref[group]).astype(bf16)
                done_ref[0, :, wide:] = dot(grad_att_t[...], context_refs[at][1 - place]).astype(
                    bf16
                )


def attend_back(
    tokens, grad_att, grad_one, projected, probs, contexts, weights, out_weights, heads, tile=256
):
    wide = weights[0].shape[0] - 16
    deep = contexts[0].shape[2]
    rows, width = grad_att.shape
    head_dim = wide // (3 * heads)
    groups = len(weights)
    parts = len(projected)
    tiles = rows // tile

    def row(n):
        return pl.BlockSpec((tile, n), lambda i: (jnp.minimum(i, tiles - 1), 0))

    def by_group(count, columns):
        return pl.BlockSpec((count, tile, columns), lambda i: (0, jnp.minimum(i, tiles - 1), 0))

    def done(skip):
        return pl.BlockSpec(
            (1, width, wide + deep), lambda i: (jnp.clip(i - skip, 0, parts - 1), 0, 0)
        )

    def stay(*shape):
        return pl.BlockSpec(shape, lambda *_: (0,) * len(shape), pipeline_mode=pl.Buffered(1))

    inputs = [
        tokens,
        grad_att,
        grad_one,
        *projected,
        *probs,
        *contexts,
        *weights,
        *out_weights,
    ]
    return pl.pallas_call(
        functools.partial(attend_back_kernel, heads, head_dim, parts, groups, tiles),
        grid=(tiles + groups,),
        in_specs=[row(width), row(width), row(width)]
        + [by_group(x.shape[0], wide) for x in projected]
        + [by_group(x.shape[0], SEQ) for x in probs]
        + [stay(*x.shape) for x in contexts]
        + [stay(*x.shape) for x in weights]
        + [stay(*x.shape) for x in out_weights],
        out_specs=[row(width), whole(8, wide), done(tiles), done(tiles + parts)],
        out_shape=[
            shape_of(f32, rows, width),
            shape_of(f32, 8, wide),
            shape_of(bf16, parts, width, wide + deep),
            shape_of(bf16, parts, width, wide + deep),
        ],
        scratch_shapes=[
            pltpu.VMEM((groups, rows, wide), bf16),
            pltpu.VMEM((groups, tile, deep), bf16),
            pltpu.VMEM((width, rows), bf16),
            pltpu.VMEM((width, rows), bf16),
        ],
        compiler_params=params(ROOM),
        cost_estimate=cost(groups * rows * wide * (width * 4 // 3 + 10 * SEQ), 8 * groups * rows * wide),
        name="attend_back",
    )(*inputs)


def small_sums_kernel(heads, index_ref, two_ref, *refs):
    out_ref = refs[-1]
    out_ref[...] = jnp.zeros_like(out_ref)
    count = (len(refs) - 1) // 3
    one_refs, bias_refs, heads_refs = (refs[k * count : (k + 1) * count] for k in range(3))
    width = out_ref.shape[1]
    wide = heads_refs[0].shape[1]
    out_ref[0:3] = two_ref[0:3]
    out_ref[3:6] = sum(x[0:3] for x in one_refs)
    at = 6
    for k in range(0, bias_refs[0].shape[1], width):
        out_ref[at : at + 1] = sum(x[:, k : k + width] for x in bias_refs)
        at += 1
    for k in range(heads):
        row = pl.ds(index_ref[0] ^ k, 1)
        out_ref[at + k : at + k + 1, :wide] = sum(x[row] for x in heads_refs)


def small_sums(index, two, one, bias_up, heads, head_size):
    width = two.shape[1]
    count = 6 + bias_up[0].shape[1] // width + head_size
    inputs = [two, *one, *bias_up, *heads]
    return pl.pallas_call(
        functools.partial(small_sums_kernel, head_size),
        in_specs=[pl.BlockSpec(memory_space=pltpu.SMEM)]
        + [pl.BlockSpec(memory_space=pltpu.VMEM)] * len(inputs),
        out_specs=pl.BlockSpec(memory_space=pltpu.VMEM),
        out_shape=shape_of(f32, -(-count // 8) * 8, width),
        name="small_sums",
    )(index, *inputs)


def place_kernel(count, index_ref, *refs):
    out_ref = refs[-1]
    step = pl.program_id(0)
    for k, piece_ref in enumerate(refs[:count]):

        @pl.when(step == k)
        def _():
            half = piece_ref.shape[0] // 2
            first = index_ref[pl.num_programs(0) + step]
            for n in range(2):
                at = pl.multiple_of((first ^ n) * half, half)
                out_ref[pl.ds(at, half)] = piece_ref[n * half : (n + 1) * half].astype(f32)


def place(index, pieces, before, shape, down):
    count = len(pieces)
    rows, cols = pieces[0].shape
    if down:
        out_map = lambda i, index: (index[i], 0)
    else:
        out_map = lambda i, index: (index[i] % 2, index[i] // 2)
    return pl.pallas_call(
        functools.partial(place_kernel, count),
        grid_spec=pltpu.PrefetchScalarGridSpec(
            num_scalar_prefetch=1,
            grid=(count,),
            in_specs=[pl.BlockSpec((rows, cols), lambda i, index: (0, 0))] * count
            + [pl.BlockSpec(memory_space=pl.ANY)] * len(before),
            out_specs=pl.BlockSpec((rows, cols), out_map),
        ),
        out_shape=shape_of(f32, *shape),
        input_output_aliases={count + 1: 0} if before else {},
        compiler_params=params(16),
        cost_estimate=cost(0, 6 * count * rows * cols),
        name="place",
    )(index, *pieces, *before)


class Net:
    def __init__(self, dp_size, head_size):
        self.size = dp_size * head_size
        self.index = lax.axis_index("dp") * head_size + lax.axis_index("head")
        self.head_bits = [1 << k for k in range(head_size.bit_length() - 1)]
        self.dp_bits = [head_size << k for k in range(dp_size.bit_length() - 1)]
        self.core = self.head_bits[0]
        self.orders = [
            (self.dp_bits[0], self.head_bits[-1]),
            (self.head_bits[-1], self.dp_bits[0]),
        ]
        self.rest = self.head_bits[1:-1] + self.dp_bits[1:]

    def bit(self, mask):
        return (self.index // mask) % 2

    def swap(self, values, mask):
        return lax.ppermute(values, AXES, [(i, i ^ mask) for i in range(self.size)])


class Line:
    def __init__(self):
        self.last = ()

    def __call__(self, step, *inputs):
        inputs, _ = lax.optimization_barrier((inputs, self.last))
        result = step(*inputs)
        self.last = jax.tree.leaves(result)
        return result


def after(values, others):
    return lax.optimization_barrier((values, others))[0]


def half(values, which, axis):
    part = values.shape[axis] // 2
    return lax.dynamic_slice_in_dim(values, which * part, part, axis)


def plus(left, right):
    return (left.astype(f32) + right.astype(f32)).astype(bf16)


def join(own, mine, received, axis):
    return jnp.where(
        own == 0,
        jnp.concatenate([mine, received], axis),
        jnp.concatenate([received, mine], axis),
    )


def travel(net, line, kept, received, shape, down, result):
    def add_core(kept, received):
        return [plus(kept[k], received[k]) for k in range(4)]

    pieces = []
    parts = line(add_core, kept, received)
    received = [net.swap(away, order[0]) for away, order in zip(parts[1::2], net.orders)]
    yield

    def add_first(mine, received):
        away, keep = [], []
        for color, order in enumerate(net.orders):
            own = net.bit(order[1])
            away.append(plus(half(mine[color], 1 - own, 0), half(received[color], 1 - own, 0)))
            keep.append(plus(half(mine[color], own, 0), half(received[color], own, 0)))
        return away, keep

    away, keep = line(add_first, parts[0::2], received)
    received = [net.swap(x, order[1]) for x, order in zip(away, net.orders)]
    yield

    def add_second(mine, received):
        return split(jnp.stack([plus(x, y) for x, y in zip(mine, received)]), 0)

    def split(mine, k):
        if k == len(net.rest):
            return mine, mine
        own = net.bit(net.rest[k])
        return half(mine, 1 - own, 1), half(mine, own, 1)

    away, mine = line(add_second, keep, received)
    for k, mask in enumerate(net.rest):
        received = net.swap(away, mask)
        yield
        away, mine = line(lambda x, y: split(plus(x, y), k + 1), mine, received)
    for mask in reversed(net.rest):
        received = net.swap(mine, mask)
        yield
        mine = line(lambda x, y: join(net.bit(mask), x, y, 1), mine, received)
    received = [net.swap(mine[color], order[1]) for color, order in enumerate(net.orders)]
    yield

    def join_second(mine, received):
        return [jnp.concatenate([mine[color], received[color]], 0) for color in (0, 1)]

    near = line(join_second, mine, received)
    far = [net.swap(x, order[0]) for x, order in zip(near, net.orders)]
    pieces += near + far + [net.swap(x, net.core) for x in near]
    yield
    far = line(lambda x: x, far)
    pieces += [net.swap(x, net.core) for x in far]
    yield
    whole_grad = []
    for core in (0, 1):
        index = piece_index(net, core)
        step = functools.partial(place, shape=shape, down=down)
        whole_grad = [line(step, index, pieces[4 * core : 4 * core + 4], whole_grad)]
        yield
    result += whole_grad


def travel_heads(net, line, kept, received, dp_size, finish, result):
    axis, *others = net.dp_bits
    last = net.head_bits[-1]
    own = net.bit(axis)

    def by_axis(values, which):
        rows = values.reshape(values.shape[:-2] + (dp_size // 2, 2, -1) + values.shape[-1:])
        return lax.dynamic_index_in_dim(rows, which, rows.ndim - 3, False)

    pairs = line(plus, kept, received)
    for mask in net.head_bits[1:-1]:
        pairs = pairs.reshape((pairs.shape[0] // 2, 2) + pairs.shape[1:])
        received = net.swap(pairs[:, 1], mask)
        yield
        pairs = line(lambda x, y: plus(x[:, 0], y), pairs, received)
    cut = pairs.shape[-1] // 2

    def split_core(groups):
        left, right = groups[..., :cut], groups[..., cut:]
        return [left[1], by_axis(right, 1 - own)], [left[0], by_axis(right, own)]

    away, mine = line(split_core, pairs)
    received = [net.swap(away[0], last), net.swap(away[1], axis)]
    yield

    def add_first(mine, received):
        left, right = [plus(x, y) for x, y in zip(mine, received)]
        return [by_axis(left, 1 - own), right[1]], [by_axis(left, own), right[0]]

    away, mine = line(add_first, mine, received)
    received = [net.swap(away[0], axis), net.swap(away[1], last)]
    yield

    def split(rows, k):
        if k == len(others):
            return rows, rows
        pairs = rows.reshape((rows.shape[0] // 2, 2) + rows.shape[1:])
        here = net.bit(others[k])
        return [lax.dynamic_index_in_dim(pairs, x, 1, False) for x in (1 - here, here)]

    def add_second(mine, received):
        return split(jnp.concatenate([plus(x, y) for x, y in zip(mine, received)], axis=-1), 0)

    away, mine = line(add_second, mine, received)
    for k, mask in enumerate(others):
        received = net.swap(away, mask)
        yield
        away, mine = line(lambda x, y: split(plus(x, y), k + 1), mine, received)
    result.append(line(finish, mine[0]))


def sum_everywhere(net, line, values, finish, result):
    for mask in net.head_bits + net.dp_bits:
        received = net.swap(values, mask)
        yield
        values = line(jnp.add, values, received)
    result.append(line(finish, values))


def piece_index(net, core):
    blocks, firsts = [], []
    for other in (0, 1):
        for color, (first, second) in enumerate(net.orders):
            square = 2 * (net.bit(net.core) ^ core) + color
            blocks.append(2 * square + (net.bit(first) ^ other))
            firsts.append(net.bit(second))
    return jnp.stack(blocks + firsts)


ORDER = "hduhsudhsudhsudhsudhsudhsudhudu"


def shards(
    dp_size,
    head_size,
    tokens,
    cotangent,
    w_qkv,
    bias_qv,
    w_out,
    bias_out,
    gain_one,
    beta_one,
    w_up,
    bias_up,
    w_down,
    bias_down,
    gain_two,
    beta_two,
):
    net = Net(dp_size, head_size)
    model_width = tokens.shape[1]
    ff = w_up.shape[1]
    local_heads = w_qkv.shape[1]
    head_dim = w_qkv.shape[2] // 3
    wide = 3 * local_heads * head_dim
    bias = jnp.stack([bias_qv[:, 0], jnp.zeros_like(bias_qv[:, 0]), bias_qv[:, 1]], axis=1)
    payload = jnp.concatenate(
        [
            jnp.transpose(w_qkv, (1, 2, 0)).reshape(wide, model_width),
            jnp.pad(bias.reshape(1, wide), ((0, 15), (0, model_width - wide))),
        ]
    )
    out_rows = w_out.reshape(-1, model_width)
    vectors = jnp.stack([bias_out, gain_one, beta_one, bias_down, gain_two, beta_two] + [bias_out] * 2)

    line = Line()
    attended, weights, out_weights = [], [], []
    own, own_out = payload, out_rows
    for k in range(0, head_size, 2):
        if k:
            own, own_out = net.swap(payload, k), net.swap(out_rows, k)
            own, own_out = after((own, own_out), attended)
        weights += [own, net.swap(own, net.core)]
        out_weights += [own_out, net.swap(own_out, net.core)]
        attended.append(line(functools.partial(attend, heads=local_heads), tokens, weights[k:]))
    projected, contexts, probs = zip(*attended)
    core = net.bit(net.core)
    first_bits = [net.bit(order[0]) for order in net.orders]
    index = jnp.stack([2 * (1 - core), 3 - 2 * core, 2 * core, 2 * core + 1] + first_bits)
    down_pieces, up_pieces, attn_part, total = [], [], [], []
    slope, low, unit_one, scale_one, layer_out, grad_two, grad_ffn, sums_two, sent, kept = line(
        forward,
        index,
        tokens,
        cotangent,
        contexts,
        out_weights,
        w_up,
        w_down,
        vectors,
        bias_up.reshape(1, -1),
    )
    down = travel(net, line, kept, net.swap(sent, net.core), w_down.shape, True, down_pieces)
    next(down)
    grad_one, grad_att, sums_one, grad_bias_up, sent, kept = line(
        backward, index, grad_ffn, slope, grad_two, low, unit_one, scale_one, w_up, w_down, vectors
    )
    next(down)
    sent = net.swap(after(sent, line.last), net.core)
    up = travel(net, line, kept, sent, w_up.shape, False, up_pieces)
    next(up)
    input_grad, sums_heads, sent, kept = line(
        functools.partial(attend_back, heads=local_heads),
        tokens,
        grad_att,
        grad_one,
        projected,
        probs,
        contexts,
        weights,
        out_weights,
    )
    next(down)
    next(up)
    sent = net.swap(after(sent, line.last), net.core)
    head_index = lax.axis_index("head")

    def finish_heads(rows):
        rows = rows.astype(f32)
        count = rows.shape[0]
        each = 3 * head_dim
        grad_qkv = jnp.stack([rows[:, k * each : (k + 1) * each] for k in range(local_heads)], 1)
        return grad_qkv, rows[:, wide:].T.reshape(local_heads, head_dim, count)

    def finish_sums(total):
        rows = ff // model_width
        parts = [total[k] for k in range(6)] + [total[6 : 6 + rows].reshape(-1)]
        own = lax.dynamic_index_in_dim(total[6 + rows :, :wide], head_index, 0, False)
        own = own.reshape(local_heads, 3, head_dim)
        pair = jnp.stack([own[:, 0], own[:, 2]], axis=1)
        cut = head_dim // dp_size
        return parts, lax.dynamic_slice_in_dim(pair, lax.axis_index("dp") * cut, cut, 2)

    heads = travel_heads(net, line, kept, sent, dp_size, finish_heads, attn_part)
    small = line(
        functools.partial(small_sums, head_size=head_size),
        head_index.reshape(1),
        sums_two,
        [sums_one],
        [grad_bias_up],
        [sums_heads],
    )
    sums = sum_everywhere(net, line, small, finish_sums, total)
    for task in ORDER:
        next({"d": down, "u": up, "h": heads, "s": sums}[task], None)
    for task in (up, down, heads, sums):
        for _ in task:
            pass
    grad_qkv, grad_out = attn_part[0]
    split, grad_bias_qv = total[0]
    full_down, full_up = down_pieces[0], up_pieces[0]
    return (
        layer_out,
        input_grad,
        grad_qkv,
        grad_bias_qv,
        grad_out,
        split[5],
        split[3],
        split[4],
        full_up,
        split[6],
        full_down,
        split[2],
        split[0],
        split[1],
    )


def solution(mesh):
    return jax.shard_map(
        functools.partial(shards, mesh.shape["dp"], mesh.shape["head"]),
        mesh=mesh,
        in_specs=(
            P(("dp", "head"), None),
            P(("dp", "head"), None),
            P(None, "head", None),
            P("head", None, None),
            P("head", None, None),
            P(),
            P(),
            P(),
            P(),
            P(),
            P(),
            P(),
            P(),
            P(),
        ),
        out_specs=(
            P(("dp", "head"), None),
            P(("dp", "head"), None),
            P("dp", "head", None),
            P("head", None, "dp"),
            P("head", None, "dp"),
            P(),
            P(),
            P(),
            P(),
            P(),
            P(),
            P(),
            P(),
            P(),
        ),
        check_vma=False,
    )
```

```python
import functools
import math

import jax
import jax.numpy as jnp
import numpy as np
from jax import lax
from jax.experimental import pallas as pl
from jax.experimental.pallas import tpu as pltpu
from jax.sharding import PartitionSpec as P

SEQ = 128
AXES = ("dp", "head")
f32 = jnp.float32
bf16 = jnp.bfloat16
epsilon = 1e-12
ROOM = 58

def dot(left, right, dims=(1, 0)):
    return lax.dot_general(
        left, right, (((dims[0],), (dims[1],)), ((), ())), preferred_element_type=f32
    )


def params(mib):
    return pltpu.CompilerParams(vmem_limit_bytes=mib * 1024 * 1024)


def cost(macs, moved, exps=0):
    return pl.CostEstimate(flops=1, bytes_accessed=1, transcendentals=0)


def whole(*shape):
    return pl.BlockSpec(shape, lambda *_: (0,) * len(shape))


def stay(*shape):
    return pl.BlockSpec(shape, lambda *_: (0,) * len(shape), pipeline_mode=pl.Buffered(1))


def anywhere():
    return pl.BlockSpec(memory_space=pl.ANY)


def shape_of(kind, *shape):
    return jax.ShapeDtypeStruct(shape, kind)


def column_sums(values):
    return jnp.sum(values, axis=0, keepdims=True)


def row_chunks(rows, heads, step=2 * SEQ):
    for begin in range(0, rows, step):
        yield [(at, head) for at in range(begin, begin + step, SEQ) for head in range(heads)]


def attend_kernel(heads, head_dim, parts, tokens_ref, *refs):
    weight_refs = refs[:parts]
    projected_ref, context_ref, probs_ref = refs[-3:]
    rows = tokens_ref.shape[0]
    wide = projected_ref.shape[2]
    for k, weight_ref in enumerate(weight_refs):

        @pl.when(pl.program_id(0) == k)
        def _():
            bias = weight_ref[wide : wide + 1, :wide].astype(f32)
            projected = dot(tokens_ref[...], weight_ref[:wide], (1, 1)) + bias
            projected_ref[0] = projected.astype(bf16)

    def part(start, head, which):
        at = (3 * head + which) * head_dim
        return projected_ref[0, start : start + SEQ, at : at + head_dim]

    for pairs in row_chunks(rows, heads):
        scores = [dot(part(s, h, 1), part(s, h, 0), (1, 1)) for s, h in pairs]
        exps = [jnp.exp(x - jnp.max(x, axis=0, keepdims=True)) for x in scores]
        probs = [(x * (1.0 / jnp.sum(x, axis=0, keepdims=True))).astype(bf16) for x in exps]
        for (s, h), p in zip(pairs, probs):
            probs_ref[h, s : s + SEQ] = p
        outs = [dot(p, part(s, h, 2), (0, 0)) for (s, h), p in zip(pairs, probs)]
        for k in range(0, len(pairs), heads):
            start = pairs[k][0]
            context_ref[0, start : start + SEQ] = jnp.concatenate(
                outs[k : k + heads], axis=1
            ).astype(bf16)


def attend(tokens, weights, before, heads, place):
    wide = weights[0].shape[0] - 16
    parts = len(weights)
    rows, width = tokens.shape
    head_dim = wide // (3 * heads)
    fresh = isinstance(before, int)
    groups = before if fresh else before[0].shape[0]
    before = [] if fresh else list(before)
    return pl.pallas_call(
        functools.partial(attend_kernel, heads, head_dim, parts),
        grid=(parts,),
        in_specs=[stay(rows, width)]
        + [stay(wide + 16, width)] * parts
        + [anywhere()] * len(before),
        out_specs=[
            pl.BlockSpec((1, rows, wide), lambda i: (i + place, 0, 0)),
            pl.BlockSpec((1, rows, wide // 3), lambda i: (i + place, 0, 0)),
            pl.BlockSpec((heads, rows, SEQ), lambda i: (i + place, 0, 0)),
        ],
        out_shape=[
            shape_of(bf16, groups, rows, wide),
            shape_of(bf16, groups, rows, wide // 3),
            shape_of(bf16, groups * heads, rows, SEQ),
        ],
        input_output_aliases={} if fresh else {1 + parts + k: k for k in range(3)},
        compiler_params=params(ROOM),
        cost_estimate=cost(parts * rows * wide * (width + 4 * SEQ), 4 * parts * rows * wide),
        name="attend",
    )(tokens, *weights, *before)


def normal(values):
    center = values - jnp.mean(values, axis=1, keepdims=True)
    inverse = lax.rsqrt(jnp.mean(center * center, axis=1, keepdims=True) + epsilon)
    return center * inverse, inverse


def normal_back(upstream, unit, inverse, gain):
    grad = upstream * gain
    return inverse * (
        grad
        - jnp.mean(grad, axis=1, keepdims=True)
        - unit * jnp.mean(grad * unit, axis=1, keepdims=True)
    )


def gelu_pair(values):
    spread = 0.5 + 0.5 * lax.erf(values * math.sqrt(0.5))
    density = jnp.exp2(values * values * (-0.5 * math.log2(math.e)))
    return values * spread, spread + values * (density * (1.0 / math.sqrt(2.0 * math.pi)))


def copies_between(pairs, semaphores):
    return [
        pltpu.make_async_copy(source, target, semaphores.at[k])
        for k, (source, target) in enumerate(pairs)
    ]


def half_squares(skip, half, width):
    return pl.BlockSpec((2, half, width), lambda i, *_: (jnp.clip(i - skip, 0, 1), 0, 0))


def forward_kernel(groups, tile, index_ref, tokens_ref, cot_hbm, context_ref, *refs):
    out_weight_refs, refs = refs[:groups], refs[groups:]
    w_up_ref, w_down_ref, vec_ref, bias_up_ref = refs[:4]
    slope_ref, low_hbm, unit_hbm, scale_hbm, out_hbm, grad_two_hbm, grad_ffn_hbm = refs[4:11]
    sums_ref, sent_ref, kept_ref = refs[11:14]
    low_ref, unit_ref, scale_ref, out_ref, grad_two_ref, grad_ffn_ref = refs[14:20]
    act_ref, total_ref, cot_ref, semaphores = refs[20:]
    step = pl.program_id(0)
    rows = tokens_ref.shape[0]
    vector = [vec_ref[k : k + 1] for k in range(6)]
    bias_out, gain_one, beta_one, bias_down, gain_two, beta_two = vector
    copies = copies_between(
        [
            (cot_hbm, cot_ref),
            (low_ref, low_hbm),
            (unit_ref, unit_hbm),
            (scale_ref, scale_hbm),
            (out_ref, out_hbm),
            (grad_two_ref, grad_two_hbm),
            (grad_ffn_ref, grad_ffn_hbm),
        ],
        semaphores,
    )

    @pl.when(step == 0)
    def _():
        copies[0].start()
        for start in range(0, rows, tile):
            here = slice(start, start + tile)
            attention = bias_out
            for group, weight_ref in enumerate(out_weight_refs):
                attention = attention + dot(context_ref[group, here], weight_ref[...])
            unit_one, scale_one = normal(tokens_ref[here].astype(f32) + attention)
            normed = unit_one * gain_one + beta_one
            unit_ref[here] = unit_one
            scale_ref[here] = scale_one
            low_ref[here] = normed.astype(bf16)
            total_ref[here] = normed + bias_down
        for copy in copies[1:4]:
            copy.start()

    @pl.when(step < 4)
    def _():
        cut = rows // 4
        parts = [slice(k * cut, (k + 1) * cut) for k in range(4)]
        hiddens = [dot(low_ref[here], w_up_ref[...]) + bias_up_ref[0] for here in parts]
        for here, hidden in zip(parts, hiddens):
            value, slope = gelu_pair(hidden)
            value = value.astype(bf16)
            act_ref[step, here] = value
            slope_ref[0, here] = slope.astype(bf16)
            total_ref[here] += dot(value, w_down_ref[...])

    @pl.when(step == 4)
    def _():
        copies[0].wait()
        sums = [0.0, 0.0, 0.0]
        for start in range(0, rows, tile):
            here = slice(start, start + tile)
            unit_two, scale_two = normal(total_ref[here])
            out_ref[here] = (unit_two * gain_two + beta_two).astype(bf16)
            upstream = cot_ref[here].astype(f32)
            grad_two = normal_back(upstream, unit_two, scale_two, gain_two)
            grad_two_ref[here] = grad_two
            grad_ffn = grad_two.astype(bf16)
            grad_ffn_ref[here] = grad_ffn
            terms = (upstream * unit_two, upstream, grad_ffn.astype(f32))
            sums = [x + column_sums(y) for x, y in zip(sums, terms)]
        for k in range(3):
            sums_ref[k : k + 1] = sums[k]
        for copy in copies[4:]:
            copy.start()

    for place, done_ref in enumerate((sent_ref, kept_ref)):

        @pl.when((step >= 4 + 2 * place) & (step < 6 + 2 * place))
        def _():
            square = index_ref[step - 4]
            first = index_ref[4 + step % 2]
            half = done_ref.shape[1]
            for n in range(2):
                left = act_ref[square, :, n * half : (n + 1) * half]
                done_ref[first ^ n] = dot(left, grad_ffn_ref[...], (0, 0)).astype(bf16)

    @pl.when(step == 7)
    def _():
        for copy in copies[1:]:
            copy.wait()


def forward(
    index, tokens, cotangent, context, out_weights, w_up, w_down, vectors, bias_up, tile=256
):
    rows, width = tokens.shape
    ff = w_up.shape[1]
    chunk = ff // 4
    kept = [(rows, width), (rows, width), (rows, 1)] + [(rows, width)] * 3
    kinds = [bf16, f32, f32, bf16, f32, bf16]
    return pl.pallas_call(
        functools.partial(forward_kernel, len(out_weights), tile),
        grid_spec=pltpu.PrefetchScalarGridSpec(
            num_scalar_prefetch=1,
            grid=(8,),
            in_specs=[stay(rows, width), anywhere(), stay(*context.shape)]
            + [stay(*w.shape) for w in out_weights]
            + [
                pl.BlockSpec((width, chunk), lambda i, *_: (0, jnp.minimum(i, 3))),
                pl.BlockSpec((chunk, width), lambda i, *_: (jnp.minimum(i, 3), 0)),
                stay(8, width),
                pl.BlockSpec((1, 1, chunk), lambda i, *_: (jnp.minimum(i, 3), 0, 0)),
            ],
            out_specs=[
                pl.BlockSpec((1, rows, chunk), lambda i, *_: (jnp.minimum(i, 3), 0, 0)),
                *([anywhere()] * 6),
                whole(8, width),
                half_squares(4, chunk // 2, width),
                half_squares(6, chunk // 2, width),
            ],
            scratch_shapes=[pltpu.VMEM(x, kind) for x, kind in zip(kept, kinds)]
            + [
                pltpu.VMEM((4, rows, chunk), bf16),
                pltpu.VMEM((rows, width), f32),
                pltpu.VMEM((rows, width), bf16),
                pltpu.SemaphoreType.DMA((7,)),
            ],
        ),
        out_shape=[shape_of(bf16, 4, rows, chunk)]
        + [shape_of(kind, *x) for x, kind in zip(kept, kinds)]
        + [
            shape_of(f32, 8, width),
            shape_of(bf16, 4, chunk // 2, width),
            shape_of(bf16, 4, chunk // 2, width),
        ],
        compiler_params=params(ROOM),
        cost_estimate=cost(rows * width * (3 * ff + width), 12 * rows * ff, rows * ff),
        name="forward",
    )(
        index,
        tokens,
        cotangent,
        context,
        *out_weights,
        w_up,
        w_down,
        vectors,
        bias_up.reshape(4, 1, chunk),
    )


def backward_kernel(
    tile,
    index_ref,
    grad_ffn_ref,
    slope_ref,
    w_up_ref,
    w_down_ref,
    vec_ref,
    grad_two_hbm,
    low_hbm,
    unit_hbm,
    scale_hbm,
    grad_one_hbm,
    grad_att_hbm,
    sums_ref,
    bias_ref,
    sent_ref,
    kept_ref,
    total_ref,
    low_ref,
    unit_ref,
    scale_ref,
    grad_att_ref,
    grad_pre_ref,
    turned_ref,
    semaphores,
):
    step = pl.program_id(0)
    rows = grad_ffn_ref.shape[0]
    copies = copies_between(
        [
            (grad_two_hbm, total_ref),
            (low_hbm, low_ref),
            (unit_hbm, unit_ref),
            (scale_hbm, scale_ref),
            (total_ref, grad_one_hbm),
            (grad_att_ref, grad_att_hbm),
        ],
        semaphores,
    )

    @pl.when(step == 0)
    def _():
        for copy in copies[:4]:
            copy.start()

    @pl.when(step < 4)
    def _():
        grad_pre = dot(grad_ffn_ref[...], w_down_ref[...], (1, 1)) * slope_ref[0].astype(f32)
        grad_pre = grad_pre.astype(bf16)
        grad_pre_ref[step] = grad_pre
        bias_ref[0] = column_sums(grad_pre.astype(f32))

    @pl.when(step == 0)
    def _():
        for copy in copies[:2]:
            copy.wait()

    @pl.when(step < 4)
    def _():
        total_ref[...] += dot(grad_pre_ref[step], w_up_ref[...], (1, 1))

    @pl.when(step == 1)
    def _():
        turned_ref[...] = low_ref[...].T

    @pl.when(step == 4)
    def _():
        for copy in copies[2:4]:
            copy.wait()
        sums = [0.0, 0.0, 0.0]
        for start in range(0, rows, tile):
            here = slice(start, start + tile)
            total, unit = total_ref[here], unit_ref[here]
            grad_one = normal_back(total, unit, scale_ref[here], vec_ref[1:2])
            total_ref[here] = grad_one
            grad_att = grad_one.astype(bf16)
            grad_att_ref[here] = grad_att
            terms = (total * unit, total, grad_att.astype(f32))
            sums = [x + column_sums(y) for x, y in zip(sums, terms)]
        for k in range(3):
            sums_ref[k : k + 1] = sums[k]
        for copy in copies[4:]:
            copy.start()

    for place, done_ref in enumerate((sent_ref, kept_ref)):

        @pl.when((step >= 4 + 2 * place) & (step < 6 + 2 * place))
        def _():
            square = index_ref[step - 4]
            first = index_ref[4 + step % 2]
            half = done_ref.shape[1]
            for n in range(2):
                left = turned_ref[n * half : (n + 1) * half]
                done_ref[first ^ n] = dot(left, grad_pre_ref[square]).astype(bf16)

    @pl.when(step == 7)
    def _():
        for copy in copies[4:]:
            copy.wait()


def backward(
    index, grad_ffn, slope, grad_two, low, unit, scale, w_up, w_down, vectors, tile=256
):
    rows, width = grad_ffn.shape
    ff = w_up.shape[1]
    chunk = ff // 4
    return pl.pallas_call(
        functools.partial(backward_kernel, tile),
        grid_spec=pltpu.PrefetchScalarGridSpec(
            num_scalar_prefetch=1,
            grid=(8,),
            in_specs=[
                stay(rows, width),
                pl.BlockSpec((1, rows, chunk), lambda i, *_: (jnp.minimum(i, 3), 0, 0)),
                pl.BlockSpec((width, chunk), lambda i, *_: (0, jnp.minimum(i, 3))),
                pl.BlockSpec((chunk, width), lambda i, *_: (jnp.minimum(i, 3), 0)),
                stay(8, width),
                *([anywhere()] * 4),
            ],
            out_specs=[
                anywhere(),
                anywhere(),
                whole(8, width),
                pl.BlockSpec((1, 1, chunk), lambda i, *_: (jnp.minimum(i, 3), 0, 0)),
                half_squares(4, width // 2, chunk),
                half_squares(6, width // 2, chunk),
            ],
            scratch_shapes=[
                pltpu.VMEM((rows, width), f32),
                pltpu.VMEM((rows, width), bf16),
                pltpu.VMEM((rows, width), f32),
                pltpu.VMEM((rows, 1), f32),
                pltpu.VMEM((rows, width), bf16),
                pltpu.VMEM((4, rows, chunk), bf16),
                pltpu.VMEM((width, rows), bf16),
                pltpu.SemaphoreType.DMA((6,)),
            ],
        ),
        out_shape=[
            shape_of(f32, rows, width),
            shape_of(bf16, rows, width),
            shape_of(f32, 8, width),
            shape_of(f32, 4, 1, chunk),
            shape_of(bf16, 4, width // 2, chunk),
            shape_of(bf16, 4, width // 2, chunk),
        ],
        compiler_params=params(ROOM),
        cost_estimate=cost(rows * width * 3 * ff, 10 * rows * ff),
        name="backward",
    )(index, grad_ffn, slope, w_up, w_down, vectors, grad_two, low, unit, scale)


def attend_back_kernel(
    heads,
    head_dim,
    groups,
    tokens_ref,
    grad_att_ref,
    grad_one_hbm,
    projected_ref,
    probs_ref,
    context_ref,
    *refs,
):
    weight_refs, refs = refs[:groups], refs[groups:]
    out_weight_refs, refs = refs[:groups], refs[groups:]
    input_hbm, sums_ref, sent_ref, kept_ref = refs[:4]
    grad_projected_ref, grad_context_ref, total_ref, tokens_t, grad_att_t, semaphores = refs[4:]
    step = pl.program_id(0)
    rows, wide = grad_projected_ref.shape
    order = list(range(1, groups, 2)) + list(range(0, groups, 2))
    copies = copies_between([(grad_one_hbm, total_ref), (total_ref, input_hbm)], semaphores)

    @pl.when(step == 0)
    def _():
        copies[0].start()
        sums_ref[...] = jnp.zeros_like(sums_ref)
        tokens_t[...] = tokens_ref[...].T
        grad_att_t[...] = grad_att_ref[...].T

    for k, group in enumerate(order):

        @pl.when(step == k)
        def _():
            grad_context_ref[...] = dot(
                grad_att_ref[...], out_weight_refs[group][...], (1, 1)
            ).astype(bf16)

    def part(start, head, which):
        at = (3 * head + which) * head_dim
        return projected_ref[0, start : start + SEQ, at : at + head_dim]

    def up(start, head):
        return grad_context_ref[start : start + SEQ, head * head_dim : (head + 1) * head_dim]

    def low(start, head):
        return probs_ref[head, start : start + SEQ]

    for pairs in row_chunks(rows, heads):
        grad_probs = [dot(part(s, h, 2), up(s, h), (1, 1)) for s, h in pairs]
        probs = [low(s, h).astype(f32) for s, h in pairs]
        inner = [jnp.sum(x * p, axis=0, keepdims=True) for x, p in zip(grad_probs, probs)]
        grad_scores = [(p * (x - i)).astype(bf16) for x, i, p in zip(grad_probs, inner, probs)]
        grad_v = [dot(low(s, h), up(s, h)) for s, h in pairs]
        grad_k = [dot(x, part(s, h, 0)) for x, (s, h) in zip(grad_scores, pairs)]
        grad_q = [dot(x, part(s, h, 1), (0, 0)) for x, (s, h) in zip(grad_scores, pairs)]
        for k in range(0, len(pairs), heads):
            start = pairs[k][0]
            pieces = [x for j in range(k, k + heads) for x in (grad_q[j], grad_k[j], grad_v[j])]
            grad_projected_ref[start : start + SEQ] = jnp.concatenate(pieces, axis=1).astype(bf16)

    @pl.when(step == 0)
    def _():
        copies[0].wait()

    for k, group in enumerate(order):

        @pl.when(step == k)
        def _():
            grad_projected = grad_projected_ref[...]
            sums_ref[group : group + 1] = column_sums(grad_projected.astype(f32))
            total_ref[...] += dot(grad_projected, weight_refs[group][:wide])

    @pl.when(step == groups - 1)
    def _():
        copies[1].start()

    for place, done_ref in enumerate((sent_ref, kept_ref)):

        @pl.when(step // (groups // 2) == place)
        def _():
            done_ref[0, :, :wide] = dot(tokens_t[...], grad_projected_ref[...]).astype(bf16)
            done_ref[0, :, wide:] = dot(grad_att_t[...], context_ref[0]).astype(bf16)

    @pl.when(step == groups - 1)
    def _():
        copies[1].wait()


def attend_back(
    tokens, grad_att, grad_one, projected, probs, context, weights, out_weights, heads
):
    wide = weights[0].shape[0] - 16
    deep = context.shape[2]
    rows, width = grad_att.shape
    head_dim = wide // (3 * heads)
    groups = len(weights)
    pairs = groups // 2

    def group(i):
        return jnp.where(i < pairs, 2 * i + 1, 2 * (i - pairs))

    def by_group(count, columns):
        return pl.BlockSpec((count, rows, columns), lambda i: (group(i), 0, 0))

    def done(skip):
        return pl.BlockSpec(
            (1, width, wide + deep), lambda i: (jnp.clip(i - skip, 0, pairs - 1), 0, 0)
        )

    return pl.pallas_call(
        functools.partial(attend_back_kernel, heads, head_dim, groups),
        grid=(groups,),
        in_specs=[
            stay(rows, width),
            stay(rows, width),
            anywhere(),
            by_group(1, wide),
            by_group(heads, SEQ),
            by_group(1, deep),
        ]
        + [stay(*x.shape) for x in weights]
        + [stay(*x.shape) for x in out_weights],
        out_specs=[anywhere(), whole(8, wide), done(0), done(pairs)],
        out_shape=[
            shape_of(f32, rows, width),
            shape_of(f32, 8, wide),
            shape_of(bf16, pairs, width, wide + deep),
            shape_of(bf16, pairs, width, wide + deep),
        ],
        scratch_shapes=[
            pltpu.VMEM((rows, wide), bf16),
            pltpu.VMEM((rows, deep), bf16),
            pltpu.VMEM((rows, width), f32),
            pltpu.VMEM((width, rows), bf16),
            pltpu.VMEM((width, rows), bf16),
            pltpu.SemaphoreType.DMA((2,)),
        ],
        compiler_params=params(ROOM),
        cost_estimate=cost(groups * rows * wide * (width * 4 // 3 + 10 * SEQ), 8 * groups * rows * wide),
        name="attend_back",
    )(tokens, grad_att, grad_one, projected, probs, context, *weights, *out_weights)


def small_sums_kernel(heads, index_ref, two_ref, *refs):
    out_ref = refs[-1]
    out_ref[...] = jnp.zeros_like(out_ref)
    one_refs, bias_refs, heads_refs = refs[:1], refs[1:2], refs[2:-1]
    width = out_ref.shape[1]
    wide = heads_refs[0].shape[1]
    out_ref[0:3] = two_ref[0:3]
    out_ref[3:6] = sum(x[0:3] for x in one_refs)
    at = 6
    for k in range(bias_refs[0].shape[0]):
        out_ref[at : at + 1] = bias_refs[0][k]
        at += 1
    for k in range(heads):
        row = pl.ds(index_ref[0] ^ k, 1)
        out_ref[at + k : at + k + 1, :wide] = sum(x[row] for x in heads_refs)


def small_sums(index, two, one, bias_up, heads, head_size):
    width = two.shape[1]
    count = 6 + bias_up[0].shape[0] + head_size
    inputs = [two, *one, *bias_up, *heads]
    return pl.pallas_call(
        functools.partial(small_sums_kernel, head_size),
        in_specs=[pl.BlockSpec(memory_space=pltpu.SMEM)]
        + [pl.BlockSpec(memory_space=pltpu.VMEM)] * len(inputs),
        out_specs=pl.BlockSpec(memory_space=pltpu.VMEM),
        out_shape=shape_of(f32, -(-count // 8) * 8, width),
        name="small_sums",
    )(index, *inputs)


def place_kernel(count, index_ref, *refs):
    out_ref = refs[-1]
    step = pl.program_id(0)
    for k, piece_ref in enumerate(refs[:count]):

        @pl.when(step == k)
        def _():
            half = piece_ref.shape[0] // 2
            first = index_ref[pl.num_programs(0) + step]
            for n in range(2):
                at = pl.multiple_of((first ^ n) * half, half)
                out_ref[pl.ds(at, half)] = piece_ref[n * half : (n + 1) * half].astype(f32)


def place(index, pieces, before, shape, down):
    count = len(pieces)
    rows, cols = pieces[0].shape
    if down:
        out_map = lambda i, index: (index[i], 0)
    else:
        out_map = lambda i, index: (index[i] % 2, index[i] // 2)
    return pl.pallas_call(
        functools.partial(place_kernel, count),
        grid_spec=pltpu.PrefetchScalarGridSpec(
            num_scalar_prefetch=1,
            grid=(count,),
            in_specs=[pl.BlockSpec((rows, cols), lambda i, index: (0, 0))] * count
            + [pl.BlockSpec(memory_space=pl.ANY)] * len(before),
            out_specs=pl.BlockSpec((rows, cols), out_map),
        ),
        out_shape=shape_of(f32, *shape),
        input_output_aliases={count + 1: 0} if before else {},
        compiler_params=params(16),
        cost_estimate=cost(0, 6 * count * rows * cols),
        name="place",
    )(index, *pieces, *before)


class Net:
    def __init__(self, dp_size, head_size):
        self.size = dp_size * head_size
        self.index = lax.axis_index("dp") * head_size + lax.axis_index("head")
        self.head_bits = [1 << k for k in range(head_size.bit_length() - 1)]
        self.dp_bits = [head_size << k for k in range(dp_size.bit_length() - 1)]
        self.core = self.head_bits[0]
        self.orders = [
            (self.dp_bits[0], self.head_bits[-1]),
            (self.head_bits[-1], self.dp_bits[0]),
        ]
        self.rest = self.head_bits[1:-1] + self.dp_bits[1:]

    def bit(self, mask):
        return (self.index // mask) % 2

    def swap(self, values, mask):
        return lax.ppermute(values, AXES, [(i, i ^ mask) for i in range(self.size)])


class Line:
    def __init__(self):
        self.last = ()

    def __call__(self, step, *inputs):
        inputs, _ = lax.optimization_barrier((inputs, self.last))
        result = step(*inputs)
        self.last = jax.tree.leaves(result)
        return result


def after(values, others):
    return lax.optimization_barrier((values, others))[0]


def half(values, which, axis):
    part = values.shape[axis] // 2
    return lax.dynamic_slice_in_dim(values, which * part, part, axis)


def plus(left, right):
    return (left.astype(f32) + right.astype(f32)).astype(bf16)


def join(own, mine, received, axis):
    return jnp.where(
        own == 0,
        jnp.concatenate([mine, received], axis),
        jnp.concatenate([received, mine], axis),
    )


def step_call(body, inputs, outputs, bits, name):
    return pl.pallas_call(
        body,
        in_specs=[pl.BlockSpec(memory_space=pltpu.SMEM)]
        + [pl.BlockSpec(memory_space=pltpu.VMEM)] * len(inputs),
        out_specs=[pl.BlockSpec(memory_space=pltpu.VMEM)] * len(outputs),
        out_shape=[shape_of(bf16, *x) for x in outputs],
        compiler_params=params(32),
        cost_estimate=cost(0, 0),
        name=name,
    )(jnp.stack(bits), *inputs)


def add_parts(kept, received):
    count, rows, cols = kept.shape

    def body(bits_ref, kept_ref, received_ref, *out_refs):
        for k in range(count):
            out_refs[k][...] = plus(kept_ref[k], received_ref[k])

    return step_call(body, [kept, received], [(rows, cols)] * count, [0], "add_parts")


def add_split(mine, received, axes, bits):
    count = len(mine)

    def halved(shape, axis):
        return shape[:axis] + (shape[axis] // 2,) + shape[axis + 1 :]

    def body(bits_ref, *refs):
        for k in range(count):
            mine_ref, received_ref, away_ref, keep_ref = refs[k::count]
            axis = axes[k]
            size = mine_ref.shape[axis] // 2
            for out_ref, which in ((away_ref, 1 - bits_ref[k]), (keep_ref, bits_ref[k])):
                here = (slice(None),) * axis + (pl.ds(which * size, size),)
                out_ref[...] = plus(mine_ref[here], received_ref[here])

    shapes = [halved(x.shape, axis) for x, axis in zip(mine, axes)]
    done = step_call(body, [*mine, *received], shapes * 2, bits, "add_split")
    return done[:count], done[count:]


def add_whole(mine, received):
    def body(bits_ref, mine_ref, received_ref, out_ref):
        out_ref[...] = plus(mine_ref[...], received_ref[...])

    return step_call(body, [mine, received], [mine.shape], [0], "add_whole")[0]


def join(mine, received, axis, bit):
    shape = mine.shape[:axis] + (2 * mine.shape[axis],) + mine.shape[axis + 1 :]

    def body(bits_ref, mine_ref, received_ref, out_ref):
        size = mine_ref.shape[axis]
        for ref, which in ((mine_ref, bits_ref[0]), (received_ref, 1 - bits_ref[0])):
            here = (slice(None),) * axis + (pl.ds(which * size, size),)
            out_ref[here] = ref[...]

    return step_call(body, [mine, received], [shape], [bit], "join")[0]


def travel(net, line, kept, received, shape, down, result):
    pieces = []
    rows, cols = kept.shape[1:]
    small = 1 << len(net.rest)
    parts = line(add_parts, kept, received)
    received = [net.swap(away, order[0]) for away, order in zip(parts[1::2], net.orders)]
    yield

    def add_first(mine, received):
        mine, received = (
            [x.reshape(2 * small, rows // (2 * small), cols) for x in y] for y in (mine, received)
        )
        return add_split(mine, received, [0, 0], [net.bit(order[1]) for order in net.orders])

    away, mine = line(add_first, parts[0::2], received)
    received = [net.swap(x, order[1]) for x, order in zip(away, net.orders)]
    yield

    def add_second(mine, received):
        if not net.rest:
            return mine, [add_whole(x, y) for x, y in zip(mine, received)]
        return add_split(mine, received, [0, 0], [net.bit(net.rest[0])] * 2)

    away, mine = line(add_second, mine, received)
    for k, mask in enumerate(net.rest):
        away = away if k else jnp.stack(away)
        mine = mine if k else jnp.stack(mine)
        received = net.swap(away, mask)
        yield
        if k + 1 < len(net.rest):
            bit = net.bit(net.rest[k + 1])
            (away,), (mine,) = line(
                lambda x, y: add_split([x], [y], [1], [bit]), mine, received
            )
        else:
            mine = line(add_whole, mine, received)
    for mask in reversed(net.rest):
        received = net.swap(mine, mask)
        yield
        mine = line(lambda x, y: join(x, y, 1, net.bit(mask)), mine, received)
    mine = [mine[color] for color in (0, 1)]
    received = [net.swap(mine[color], order[1]) for color, order in enumerate(net.orders)]
    yield

    def join_second(mine, received):
        return [join(x, y, 0, 0 * net.bit(net.core)) for x, y in zip(mine, received)]

    near = [x.reshape(rows, cols) for x in line(join_second, mine, received)]
    far = [net.swap(x, order[0]) for x, order in zip(near, net.orders)]
    pieces += near + far + [net.swap(x, net.core) for x in near]
    yield
    pieces += [net.swap(x, net.core) for x in far]
    whole_grad = []
    for core in (0, 1):
        index = piece_index(net, core)
        step = functools.partial(place, shape=shape, down=down)
        whole_grad = [line(step, index, pieces[4 * core : 4 * core + 4], whole_grad)]
        yield
    result += whole_grad


def travel_heads(net, line, kept, received, dp_size, finish, result):
    axis, *others = net.dp_bits
    last = net.head_bits[-1]
    own = net.bit(axis)
    for mask in net.head_bits[1:-1]:
        pairs = line(plus, kept, received)
        pairs = pairs.reshape((pairs.shape[0] // 2, 2) + pairs.shape[1:])
        kept, received = pairs[:, 0], net.swap(pairs[:, 1], mask)
        yield
    _, rows, cols = kept.shape
    each = rows // dp_size
    cut = cols // 2

    def add_core(kept, received):
        def body(bits_ref, kept_ref, received_ref, *out_refs):
            left = [plus(kept_ref[k, ..., :cut], received_ref[k, ..., :cut]) for k in (1, 0)]
            for out_ref, value in zip(out_refs, left):
                out_ref[...] = value
            for out_ref, which in zip(out_refs[2:], (1 - bits_ref[0], bits_ref[0])):
                for n in range(dp_size // 2):
                    here = (slice(None), 2 * n + which, slice(None), slice(cut, None))
                    out_ref[:, n] = plus(kept_ref[here], received_ref[here])

        kept, received = (x.reshape(2, dp_size, each, cols) for x in (kept, received))
        shapes = [(dp_size, each, cut)] * 2 + [(2, dp_size // 2, each, cut)] * 2
        return step_call(body, [kept, received], shapes, [own], "add_core")

    away_left, left, away_right, right = line(add_core, kept, received)
    received = [net.swap(away_left, last), net.swap(away_right, axis)]
    yield

    def add_first(left, right, received):
        def body(bits_ref, left_ref, right_ref, other_left_ref, other_right_ref, *out_refs):
            for out_ref, which in zip(out_refs, (1 - bits_ref[0], bits_ref[0])):
                for n in range(dp_size // 2):
                    out_ref[n] = plus(left_ref[2 * n + which], other_left_ref[2 * n + which])
            for out_ref, which in zip(out_refs[2:], (1, 0)):
                out_ref[...] = plus(right_ref[which], other_right_ref[which])

        shapes = [(dp_size // 2, each, cut)] * 4
        return step_call(body, [left, right, *received], shapes, [own], "add_first")

    away_left, left, away_right, right = line(add_first, left, right, received)
    received = [net.swap(away_left, axis), net.swap(away_right, last)]
    yield

    def add_second(left, right, received):
        def body(bits_ref, left_ref, right_ref, other_left_ref, other_right_ref, *out_refs):
            for out_ref, which in zip(out_refs, (1 - bits_ref[0], bits_ref[0])):
                size = out_ref.shape[0]
                here = pl.ds(which * size, size)
                out_ref[..., :cut] = plus(left_ref[here], other_left_ref[here])
                out_ref[..., cut:] = plus(right_ref[here], other_right_ref[here])

        shapes = [(dp_size // 4, each, cols)] * 2
        return step_call(
            body, [left, right, *received], shapes, [net.bit(others[-1])], "add_second"
        )

    away, mine = line(add_second, left, right, received)
    for k, mask in enumerate(reversed(others)):
        received = net.swap(away, mask)
        yield
        if k + 1 < len(others):
            bit = net.bit(others[-2 - k])
            (away,), (mine,) = line(
                lambda x, y: add_split([x], [y], [0], [bit]), mine, received
            )
    result.append(line(lambda x, y: finish(plus(x[0], y[0])), mine, received))


def add_sums(values, received):
    def body(values_ref, received_ref, out_ref):
        out_ref[...] = values_ref[...] + received_ref[...]

    return pl.pallas_call(
        body,
        out_shape=shape_of(f32, *values.shape),
        cost_estimate=cost(0, 0),
        name="add_sums",
    )(values, received)


def sum_everywhere(net, line, values, finish, result):
    for mask in net.head_bits + net.dp_bits:
        received = net.swap(values, mask)
        yield
        values = line(jnp.add, values, received)
    result.append(line(finish, values))


def piece_index(net, core):
    blocks, firsts = [], []
    for other in (0, 1):
        for color, (first, second) in enumerate(net.orders):
            square = 2 * (net.bit(net.core) ^ core) + color
            blocks.append(2 * square + (net.bit(first) ^ other))
            firsts.append(net.bit(second))
    return jnp.stack(blocks + firsts)


ORDER = "dBdUuAudHhusduhdsudhsudhsudhsuduuuu"


def shards(
    dp_size,
    head_size,
    tokens,
    cotangent,
    w_qkv,
    bias_qv,
    w_out,
    bias_out,
    gain_one,
    beta_one,
    w_up,
    bias_up,
    w_down,
    bias_down,
    gain_two,
    beta_two,
):
    net = Net(dp_size, head_size)
    model_width = tokens.shape[1]
    ff = w_up.shape[1]
    local_heads = w_qkv.shape[1]
    head_dim = w_qkv.shape[2] // 3
    wide = 3 * local_heads * head_dim
    scale = np.array([float(head_dim) ** -0.5, 1.0, 1.0], np.float32)
    bias = jnp.stack([bias_qv[:, 0], jnp.zeros_like(bias_qv[:, 0]), bias_qv[:, 1]], axis=1)
    scale_rows = jnp.asarray(np.repeat(np.tile(scale, local_heads), head_dim), bf16)
    payload = jnp.concatenate(
        [
            jnp.transpose(w_qkv, (1, 2, 0)).reshape(wide, model_width) * scale_rows[:, None],
            jnp.pad(
                (bias.reshape(wide) * scale_rows)[None], ((0, 15), (0, model_width - wide))
            ),
        ]
    )
    out_rows = w_out.reshape(-1, model_width)
    vectors = jnp.stack([bias_out, gain_one, beta_one, bias_down, gain_two, beta_two] + [bias_out] * 2)

    line = Line()
    attended, weights, out_weights = head_size, [], []
    for k in range(0, head_size, 2):
        own, own_out = payload, out_rows
        if k:
            own = after(net.swap(payload, k), attended)
            own_out = net.swap(after(out_rows, own), k)
        weights += [own, net.swap(own, net.core)]
        step = functools.partial(attend, heads=local_heads, place=k)
        if k:
            attended = line(step, tokens, weights[k:], attended)
            own_out = after(own_out, attended)
        else:
            attended = line(functools.partial(step, before=head_size), tokens, weights)
        out_weights += [own_out, net.swap(own_out, net.core)]
    projected, context, probs = attended
    core = net.bit(net.core)
    first_bits = [net.bit(order[0]) for order in net.orders]
    index = jnp.stack([2 * (1 - core), 3 - 2 * core, 2 * core, 2 * core + 1] + first_bits)
    down_pieces, up_pieces, attn_part, total = [], [], [], []
    slope, low, unit_one, scale_one, layer_out, grad_two, grad_ffn, sums_two, sent, kept = line(
        forward,
        index,
        tokens,
        cotangent,
        context,
        out_weights,
        w_up,
        w_down,
        vectors,
        bias_up.reshape(1, -1),
    )
    head_index = lax.axis_index("head")

    def finish_heads(rows):
        rows = rows.astype(f32)
        count = rows.shape[0]
        each = 3 * head_dim
        factor = jnp.asarray(np.repeat(scale, head_dim))
        grad_qkv = jnp.stack([rows[:, k * each : (k + 1) * each] * factor for k in range(local_heads)], 1)
        return grad_qkv, rows[:, wide:].T.reshape(local_heads, head_dim, count)

    def finish_sums(total):
        rows = ff // model_width
        parts = [total[k] for k in range(6)] + [total[6 : 6 + rows].reshape(-1)]
        own = lax.dynamic_index_in_dim(total[6 + rows :, :wide], head_index, 0, False)
        own = own.reshape(local_heads, 3, head_dim)
        pair = jnp.stack([own[:, 0] * scale[0], own[:, 2]], axis=1)
        cut = head_dim // dp_size
        return parts, lax.dynamic_slice_in_dim(pair, lax.axis_index("dp") * cut, cut, 2)

    tasks = {
        "d": travel(net, line, kept, net.swap(sent, net.core), w_down.shape, True, down_pieces)
    }
    for step in ORDER:
        if step == "B":
            grad_one, grad_att, sums_one, grad_bias_up, sent, kept = line(
                backward,
                index,
                grad_ffn,
                slope,
                grad_two,
                low,
                unit_one,
                scale_one,
                w_up,
                w_down,
                vectors,
            )
        elif step == "U":
            sent = net.swap(after(sent, line.last), net.core)
            tasks["u"] = travel(net, line, kept, sent, w_up.shape, False, up_pieces)
        elif step == "A":
            input_grad, sums_heads, sent, kept = line(
                functools.partial(attend_back, heads=local_heads),
                tokens,
                grad_att,
                grad_one,
                projected,
                probs,
                context,
                weights,
                out_weights,
            )
        elif step == "H":
            sent = net.swap(after(sent, line.last), net.core)
            tasks["h"] = travel_heads(net, line, kept, sent, dp_size, finish_heads, attn_part)
        elif step == "s" and "s" not in tasks:
            small = line(
                functools.partial(small_sums, head_size=head_size),
                head_index.reshape(1),
                sums_two,
                [sums_one],
                [grad_bias_up],
                [sums_heads],
            )
            tasks["s"] = sum_everywhere(net, line, small, finish_sums, total)
            next(tasks["s"])
        else:
            next(tasks[step], None)
    for task in tasks.values():
        for _ in task:
            pass
    grad_qkv, grad_out = attn_part[0]
    split, grad_bias_qv = total[0]
    full_down, full_up = down_pieces[0], up_pieces[0]
    return (
        layer_out,
        input_grad,
        grad_qkv,
        grad_bias_qv,
        grad_out,
        split[5],
        split[3],
        split[4],
        full_up,
        split[6],
        full_down,
        split[2],
        split[0],
        split[1],
    )


def solution(mesh):
    return jax.shard_map(
        functools.partial(shards, mesh.shape["dp"], mesh.shape["head"]),
        mesh=mesh,
        in_specs=(
            P(("dp", "head"), None),
            P(("dp", "head"), None),
            P(None, "head", None),
            P("head", None, None),
            P("head", None, None),
            P(),
            P(),
            P(),
            P(),
            P(),
            P(),
            P(),
            P(),
            P(),
        ),
        out_specs=(
            P(("dp", "head"), None),
            P(("dp", "head"), None),
            P("dp", "head", None),
            P("head", None, "dp"),
            P("head", None, "dp"),
            P(),
            P(),
            P(),
            P(),
            P(),
            P(),
            P(),
            P(),
            P(),
        ),
        check_vma=False,
    )
```

```python
import functools
import math

import jax
import jax.numpy as jnp
import numpy as np
from jax import lax
from jax.experimental import pallas as pl
from jax.experimental.pallas import tpu as pltpu
from jax.sharding import PartitionSpec as P

SEQ = 128
AXES = ("dp", "head")
f32 = jnp.float32
bf16 = jnp.bfloat16
epsilon = 1e-12
ROOM = 58

def dot(left, right, dims=(1, 0)):
    return lax.dot_general(
        left, right, (((dims[0],), (dims[1],)), ((), ())), preferred_element_type=f32
    )


def params(mib):
    return pltpu.CompilerParams(vmem_limit_bytes=mib * 1024 * 1024)


def cost(macs, moved, exps=0):
    return pl.CostEstimate(flops=1, bytes_accessed=1, transcendentals=0)


def whole(*shape):
    return pl.BlockSpec(shape, lambda *_: (0,) * len(shape))


def stay(*shape):
    return pl.BlockSpec(shape, lambda *_: (0,) * len(shape), pipeline_mode=pl.Buffered(1))


def anywhere():
    return pl.BlockSpec(memory_space=pl.ANY)


def shape_of(kind, *shape):
    return jax.ShapeDtypeStruct(shape, kind)


def column_sums(values):
    return jnp.sum(values, axis=0, keepdims=True)


def row_chunks(rows, heads, step=2 * SEQ):
    for begin in range(0, rows, step):
        yield [(at, head) for at in range(begin, begin + step, SEQ) for head in range(heads)]


def attend_kernel(heads, head_dim, parts, tokens_ref, *refs):
    weight_refs = refs[:parts]
    projected_ref, context_ref, probs_ref = refs[-3:]
    rows = tokens_ref.shape[0]
    wide = projected_ref.shape[2]
    for k, weight_ref in enumerate(weight_refs):

        @pl.when(pl.program_id(0) == k)
        def _():
            bias = weight_ref[wide : wide + 1, :wide].astype(f32)
            projected = dot(tokens_ref[...], weight_ref[:wide], (1, 1)) + bias
            projected_ref[0] = projected.astype(bf16)

    def part(start, head, which):
        at = (3 * head + which) * head_dim
        return projected_ref[0, start : start + SEQ, at : at + head_dim]

    for pairs in row_chunks(rows, heads):
        scores = [dot(part(s, h, 1), part(s, h, 0), (1, 1)) for s, h in pairs]
        exps = [jnp.exp(x - jnp.max(x, axis=0, keepdims=True)) for x in scores]
        probs = [(x * (1.0 / jnp.sum(x, axis=0, keepdims=True))).astype(bf16) for x in exps]
        for (s, h), p in zip(pairs, probs):
            probs_ref[h, s : s + SEQ] = p
        outs = [dot(p, part(s, h, 2), (0, 0)) for (s, h), p in zip(pairs, probs)]
        for k in range(0, len(pairs), heads):
            start = pairs[k][0]
            context_ref[0, start : start + SEQ] = jnp.concatenate(
                outs[k : k + heads], axis=1
            ).astype(bf16)


def attend(tokens, weights, before, heads, place):
    wide = weights[0].shape[0] - 16
    parts = len(weights)
    rows, width = tokens.shape
    head_dim = wide // (3 * heads)
    fresh = isinstance(before, int)
    groups = before if fresh else before[0].shape[0]
    before = [] if fresh else list(before)
    return pl.pallas_call(
        functools.partial(attend_kernel, heads, head_dim, parts),
        grid=(parts,),
        in_specs=[stay(rows, width)]
        + [stay(wide + 16, width)] * parts
        + [anywhere()] * len(before),
        out_specs=[
            pl.BlockSpec((1, rows, wide), lambda i: (i + place, 0, 0)),
            pl.BlockSpec((1, rows, wide // 3), lambda i: (i + place, 0, 0)),
            pl.BlockSpec((heads, rows, SEQ), lambda i: (i + place, 0, 0)),
        ],
        out_shape=[
            shape_of(bf16, groups, rows, wide),
            shape_of(bf16, groups, rows, wide // 3),
            shape_of(bf16, groups * heads, rows, SEQ),
        ],
        input_output_aliases={} if fresh else {1 + parts + k: k for k in range(3)},
        compiler_params=params(ROOM),
        cost_estimate=cost(parts * rows * wide * (width + 4 * SEQ), 4 * parts * rows * wide),
        name="attend",
    )(tokens, *weights, *before)


def normal(values):
    center = values - jnp.mean(values, axis=1, keepdims=True)
    inverse = lax.rsqrt(jnp.mean(center * center, axis=1, keepdims=True) + epsilon)
    return center * inverse, inverse


def normal_back(upstream, unit, inverse, gain):
    grad = upstream * gain
    return inverse * (
        grad
        - jnp.mean(grad, axis=1, keepdims=True)
        - unit * jnp.mean(grad * unit, axis=1, keepdims=True)
    )


def gelu_pair(values):
    spread = 0.5 + 0.5 * lax.erf(values * math.sqrt(0.5))
    density = jnp.exp2(values * values * (-0.5 * math.log2(math.e)))
    return values * spread, spread + values * (density * (1.0 / math.sqrt(2.0 * math.pi)))


def copies_between(pairs, semaphores):
    return [
        pltpu.make_async_copy(source, target, semaphores.at[k])
        for k, (source, target) in enumerate(pairs)
    ]


def half_squares(skip, half, width):
    return pl.BlockSpec((2, half, width), lambda i, *_: (jnp.clip(i - skip, 0, 1), 0, 0))


def forward_kernel(groups, tile, index_ref, tokens_ref, cot_hbm, context_ref, *refs):
    out_weight_refs, refs = refs[:groups], refs[groups:]
    w_up_ref, w_down_ref, vec_ref, bias_up_ref = refs[:4]
    slope_ref, low_hbm, unit_hbm, scale_hbm, out_hbm, grad_two_hbm, grad_ffn_hbm = refs[4:11]
    sums_ref, sent_ref, kept_ref = refs[11:14]
    low_ref, unit_ref, scale_ref, out_ref, grad_two_ref, grad_ffn_ref = refs[14:20]
    act_ref, total_ref, cot_ref, semaphores = refs[20:]
    step = pl.program_id(0)
    rows = tokens_ref.shape[0]
    vector = [vec_ref[k : k + 1] for k in range(6)]
    bias_out, gain_one, beta_one, bias_down, gain_two, beta_two = vector
    copies = copies_between(
        [
            (cot_hbm, cot_ref),
            (low_ref, low_hbm),
            (unit_ref, unit_hbm),
            (scale_ref, scale_hbm),
            (out_ref, out_hbm),
            (grad_two_ref, grad_two_hbm),
            (grad_ffn_ref, grad_ffn_hbm),
        ],
        semaphores,
    )

    @pl.when(step == 0)
    def _():
        copies[0].start()
        for start in range(0, rows, tile):
            here = slice(start, start + tile)
            attention = bias_out
            for group, weight_ref in enumerate(out_weight_refs):
                attention = attention + dot(context_ref[group, here], weight_ref[...])
            unit_one, scale_one = normal(tokens_ref[here].astype(f32) + attention)
            normed = unit_one * gain_one + beta_one
            unit_ref[here] = unit_one
            scale_ref[here] = scale_one
            low_ref[here] = normed.astype(bf16)
            total_ref[here] = normed + bias_down
        for copy in copies[1:4]:
            copy.start()

    @pl.when(step < 4)
    def _():
        cut = rows // 4
        parts = [slice(k * cut, (k + 1) * cut) for k in range(4)]
        hiddens = [dot(low_ref[here], w_up_ref[...]) + bias_up_ref[0] for here in parts]
        for here, hidden in zip(parts, hiddens):
            value, slope = gelu_pair(hidden)
            value = value.astype(bf16)
            act_ref[step, here] = value
            slope_ref[0, here] = slope.astype(bf16)
            total_ref[here] += dot(value, w_down_ref[...])

    @pl.when(step == 4)
    def _():
        copies[0].wait()
        sums = [0.0, 0.0, 0.0]
        for start in range(0, rows, tile):
            here = slice(start, start + tile)
            unit_two, scale_two = normal(total_ref[here])
            out_ref[here] = (unit_two * gain_two + beta_two).astype(bf16)
            upstream = cot_ref[here].astype(f32)
            grad_two = normal_back(upstream, unit_two, scale_two, gain_two)
            grad_two_ref[here] = grad_two
            grad_ffn = grad_two.astype(bf16)
            grad_ffn_ref[here] = grad_ffn
            terms = (upstream * unit_two, upstream, grad_ffn.astype(f32))
            sums = [x + column_sums(y) for x, y in zip(sums, terms)]
        for k in range(3):
            sums_ref[k : k + 1] = sums[k]
        for copy in copies[4:]:
            copy.start()

    for place, done_ref in enumerate((sent_ref, kept_ref)):

        @pl.when((step >= 4 + 2 * place) & (step < 6 + 2 * place))
        def _():
            square = index_ref[step - 4]
            first = index_ref[4 + step % 2]
            half = done_ref.shape[1]
            for n in range(2):
                left = act_ref[square, :, n * half : (n + 1) * half]
                done_ref[first ^ n] = dot(left, grad_ffn_ref[...], (0, 0)).astype(bf16)

    @pl.when(step == 7)
    def _():
        for copy in copies[1:]:
            copy.wait()


def forward(
    index, tokens, cotangent, context, out_weights, w_up, w_down, vectors, bias_up, tile=256
):
    rows, width = tokens.shape
    ff = w_up.shape[1]
    chunk = ff // 4
    kept = [(rows, width), (rows, width), (rows, 1)] + [(rows, width)] * 3
    kinds = [bf16, f32, f32, bf16, f32, bf16]
    return pl.pallas_call(
        functools.partial(forward_kernel, len(out_weights), tile),
        grid_spec=pltpu.PrefetchScalarGridSpec(
            num_scalar_prefetch=1,
            grid=(8,),
            in_specs=[stay(rows, width), anywhere(), stay(*context.shape)]
            + [stay(*w.shape) for w in out_weights]
            + [
                pl.BlockSpec((width, chunk), lambda i, *_: (0, jnp.minimum(i, 3))),
                pl.BlockSpec((chunk, width), lambda i, *_: (jnp.minimum(i, 3), 0)),
                stay(8, width),
                pl.BlockSpec((1, 1, chunk), lambda i, *_: (jnp.minimum(i, 3), 0, 0)),
            ],
            out_specs=[
                pl.BlockSpec((1, rows, chunk), lambda i, *_: (jnp.minimum(i, 3), 0, 0)),
                *([anywhere()] * 6),
                whole(8, width),
                half_squares(4, chunk // 2, width),
                half_squares(6, chunk // 2, width),
            ],
            scratch_shapes=[pltpu.VMEM(x, kind) for x, kind in zip(kept, kinds)]
            + [
                pltpu.VMEM((4, rows, chunk), bf16),
                pltpu.VMEM((rows, width), f32),
                pltpu.VMEM((rows, width), bf16),
                pltpu.SemaphoreType.DMA((7,)),
            ],
        ),
        out_shape=[shape_of(bf16, 4, rows, chunk)]
        + [shape_of(kind, *x) for x, kind in zip(kept, kinds)]
        + [
            shape_of(f32, 8, width),
            shape_of(bf16, 4, chunk // 2, width),
            shape_of(bf16, 4, chunk // 2, width),
        ],
        compiler_params=params(ROOM),
        cost_estimate=cost(rows * width * (3 * ff + width), 12 * rows * ff, rows * ff),
        name="forward",
    )(
        index,
        tokens,
        cotangent,
        context,
        *out_weights,
        w_up,
        w_down,
        vectors,
        bias_up.reshape(4, 1, chunk),
    )


def backward_kernel(
    tile,
    index_ref,
    grad_ffn_ref,
    slope_ref,
    w_up_ref,
    w_down_ref,
    vec_ref,
    grad_two_hbm,
    low_hbm,
    unit_hbm,
    scale_hbm,
    grad_one_hbm,
    grad_att_hbm,
    sums_ref,
    bias_ref,
    sent_ref,
    kept_ref,
    total_ref,
    low_ref,
    unit_ref,
    scale_ref,
    grad_att_ref,
    grad_pre_ref,
    turned_ref,
    semaphores,
):
    step = pl.program_id(0)
    rows = grad_ffn_ref.shape[0]
    copies = copies_between(
        [
            (grad_two_hbm, total_ref),
            (low_hbm, low_ref),
            (unit_hbm, unit_ref),
            (scale_hbm, scale_ref),
            (total_ref, grad_one_hbm),
            (grad_att_ref, grad_att_hbm),
        ],
        semaphores,
    )

    @pl.when(step == 0)
    def _():
        for copy in copies[:4]:
            copy.start()

    @pl.when(step < 4)
    def _():
        grad_pre = dot(grad_ffn_ref[...], w_down_ref[...], (1, 1)) * slope_ref[0].astype(f32)
        grad_pre = grad_pre.astype(bf16)
        grad_pre_ref[step] = grad_pre
        bias_ref[0] = column_sums(grad_pre.astype(f32))

    @pl.when(step == 0)
    def _():
        for copy in copies[:2]:
            copy.wait()

    @pl.when(step < 4)
    def _():
        total_ref[...] += dot(grad_pre_ref[step], w_up_ref[...], (1, 1))

    @pl.when(step == 1)
    def _():
        turned_ref[...] = low_ref[...].T

    @pl.when(step == 4)
    def _():
        for copy in copies[2:4]:
            copy.wait()
        sums = [0.0, 0.0, 0.0]
        for start in range(0, rows, tile):
            here = slice(start, start + tile)
            total, unit = total_ref[here], unit_ref[here]
            grad_one = normal_back(total, unit, scale_ref[here], vec_ref[1:2])
            total_ref[here] = grad_one
            grad_att = grad_one.astype(bf16)
            grad_att_ref[here] = grad_att
            terms = (total * unit, total, grad_att.astype(f32))
            sums = [x + column_sums(y) for x, y in zip(sums, terms)]
        for k in range(3):
            sums_ref[k : k + 1] = sums[k]
        for copy in copies[4:]:
            copy.start()

    for place, done_ref in enumerate((sent_ref, kept_ref)):

        @pl.when((step >= 4 + 2 * place) & (step < 6 + 2 * place))
        def _():
            square = index_ref[step - 4]
            first = index_ref[4 + step % 2]
            half = done_ref.shape[1]
            for n in range(2):
                left = turned_ref[n * half : (n + 1) * half]
                done_ref[first ^ n] = dot(left, grad_pre_ref[square]).astype(bf16)

    @pl.when(step == 7)
    def _():
        for copy in copies[4:]:
            copy.wait()


def backward(
    index, grad_ffn, slope, grad_two, low, unit, scale, w_up, w_down, vectors, tile=256
):
    rows, width = grad_ffn.shape
    ff = w_up.shape[1]
    chunk = ff // 4
    return pl.pallas_call(
        functools.partial(backward_kernel, tile),
        grid_spec=pltpu.PrefetchScalarGridSpec(
            num_scalar_prefetch=1,
            grid=(8,),
            in_specs=[
                stay(rows, width),
                pl.BlockSpec((1, rows, chunk), lambda i, *_: (jnp.minimum(i, 3), 0, 0)),
                pl.BlockSpec((width, chunk), lambda i, *_: (0, jnp.minimum(i, 3))),
                pl.BlockSpec((chunk, width), lambda i, *_: (jnp.minimum(i, 3), 0)),
                stay(8, width),
                *([anywhere()] * 4),
            ],
            out_specs=[
                anywhere(),
                anywhere(),
                whole(8, width),
                pl.BlockSpec((1, 1, chunk), lambda i, *_: (jnp.minimum(i, 3), 0, 0)),
                half_squares(4, width // 2, chunk),
                half_squares(6, width // 2, chunk),
            ],
            scratch_shapes=[
                pltpu.VMEM((rows, width), f32),
                pltpu.VMEM((rows, width), bf16),
                pltpu.VMEM((rows, width), f32),
                pltpu.VMEM((rows, 1), f32),
                pltpu.VMEM((rows, width), bf16),
                pltpu.VMEM((4, rows, chunk), bf16),
                pltpu.VMEM((width, rows), bf16),
                pltpu.SemaphoreType.DMA((6,)),
            ],
        ),
        out_shape=[
            shape_of(f32, rows, width),
            shape_of(bf16, rows, width),
            shape_of(f32, 8, width),
            shape_of(f32, 4, 1, chunk),
            shape_of(bf16, 4, width // 2, chunk),
            shape_of(bf16, 4, width // 2, chunk),
        ],
        compiler_params=params(ROOM),
        cost_estimate=cost(rows * width * 3 * ff, 10 * rows * ff),
        name="backward",
    )(index, grad_ffn, slope, w_up, w_down, vectors, grad_two, low, unit, scale)


def attend_back_kernel(
    heads,
    head_dim,
    groups,
    tokens_ref,
    grad_att_ref,
    grad_one_hbm,
    projected_ref,
    probs_ref,
    context_ref,
    *refs,
):
    weight_refs, refs = refs[:groups], refs[groups:]
    out_weight_refs, refs = refs[:groups], refs[groups:]
    input_hbm, sums_ref, sent_ref, kept_ref = refs[:4]
    grad_projected_ref, grad_context_ref, total_ref, tokens_t, grad_att_t, semaphores = refs[4:]
    step = pl.program_id(0)
    rows, wide = grad_projected_ref.shape
    order = list(range(1, groups, 2)) + list(range(0, groups, 2))
    copies = copies_between([(grad_one_hbm, total_ref), (total_ref, input_hbm)], semaphores)

    @pl.when(step == 0)
    def _():
        copies[0].start()
        sums_ref[...] = jnp.zeros_like(sums_ref)
        tokens_t[...] = tokens_ref[...].T
        grad_att_t[...] = grad_att_ref[...].T

    for k, group in enumerate(order):

        @pl.when(step == k)
        def _():
            grad_context_ref[...] = dot(
                grad_att_ref[...], out_weight_refs[group][...], (1, 1)
            ).astype(bf16)

    def part(start, head, which):
        at = (3 * head + which) * head_dim
        return projected_ref[0, start : start + SEQ, at : at + head_dim]

    def up(start, head):
        return grad_context_ref[start : start + SEQ, head * head_dim : (head + 1) * head_dim]

    def low(start, head):
        return probs_ref[head, start : start + SEQ]

    for pairs in row_chunks(rows, heads):
        grad_probs = [dot(part(s, h, 2), up(s, h), (1, 1)) for s, h in pairs]
        probs = [low(s, h).astype(f32) for s, h in pairs]
        inner = [jnp.sum(x * p, axis=0, keepdims=True) for x, p in zip(grad_probs, probs)]
        grad_scores = [(p * (x - i)).astype(bf16) for x, i, p in zip(grad_probs, inner, probs)]
        grad_v = [dot(low(s, h), up(s, h)) for s, h in pairs]
        grad_k = [dot(x, part(s, h, 0)) for x, (s, h) in zip(grad_scores, pairs)]
        grad_q = [dot(x, part(s, h, 1), (0, 0)) for x, (s, h) in zip(grad_scores, pairs)]
        for k in range(0, len(pairs), heads):
            start = pairs[k][0]
            pieces = [x for j in range(k, k + heads) for x in (grad_q[j], grad_k[j], grad_v[j])]
            grad_projected_ref[start : start + SEQ] = jnp.concatenate(pieces, axis=1).astype(bf16)

    @pl.when(step == 0)
    def _():
        copies[0].wait()

    for k, group in enumerate(order):

        @pl.when(step == k)
        def _():
            grad_projected = grad_projected_ref[...]
            sums_ref[group : group + 1] = column_sums(grad_projected.astype(f32))
            total_ref[...] += dot(grad_projected, weight_refs[group][:wide])

    @pl.when(step == groups - 1)
    def _():
        copies[1].start()

    for place, done_ref in enumerate((sent_ref, kept_ref)):

        @pl.when(step // (groups // 2) == place)
        def _():
            done_ref[0, :, :wide] = dot(tokens_t[...], grad_projected_ref[...]).astype(bf16)
            done_ref[0, :, wide:] = dot(grad_att_t[...], context_ref[0]).astype(bf16)

    @pl.when(step == groups - 1)
    def _():
        copies[1].wait()


def attend_back(
    tokens, grad_att, grad_one, projected, probs, context, weights, out_weights, heads
):
    wide = weights[0].shape[0] - 16
    deep = context.shape[2]
    rows, width = grad_att.shape
    head_dim = wide // (3 * heads)
    groups = len(weights)
    pairs = groups // 2

    def group(i):
        return jnp.where(i < pairs, 2 * i + 1, 2 * (i - pairs))

    def by_group(count, columns):
        return pl.BlockSpec((count, rows, columns), lambda i: (group(i), 0, 0))

    def done(skip):
        return pl.BlockSpec(
            (1, width, wide + deep), lambda i: (jnp.clip(i - skip, 0, pairs - 1), 0, 0)
        )

    return pl.pallas_call(
        functools.partial(attend_back_kernel, heads, head_dim, groups),
        grid=(groups,),
        in_specs=[
            stay(rows, width),
            stay(rows, width),
            anywhere(),
            by_group(1, wide),
            by_group(heads, SEQ),
            by_group(1, deep),
        ]
        + [stay(*x.shape) for x in weights]
        + [stay(*x.shape) for x in out_weights],
        out_specs=[anywhere(), whole(8, wide), done(0), done(pairs)],
        out_shape=[
            shape_of(f32, rows, width),
            shape_of(f32, 8, wide),
            shape_of(bf16, pairs, width, wide + deep),
            shape_of(bf16, pairs, width, wide + deep),
        ],
        scratch_shapes=[
            pltpu.VMEM((rows, wide), bf16),
            pltpu.VMEM((rows, deep), bf16),
            pltpu.VMEM((rows, width), f32),
            pltpu.VMEM((width, rows), bf16),
            pltpu.VMEM((width, rows), bf16),
            pltpu.SemaphoreType.DMA((2,)),
        ],
        compiler_params=params(ROOM),
        cost_estimate=cost(groups * rows * wide * (width * 4 // 3 + 10 * SEQ), 8 * groups * rows * wide),
        name="attend_back",
    )(tokens, grad_att, grad_one, projected, probs, context, *weights, *out_weights)


def small_sums_kernel(heads, index_ref, two_ref, *refs):
    out_ref = refs[-1]
    out_ref[...] = jnp.zeros_like(out_ref)
    one_refs, bias_refs, heads_refs = refs[:1], refs[1:2], refs[2:-1]
    width = out_ref.shape[1]
    wide = heads_refs[0].shape[1]
    out_ref[0:3] = two_ref[0:3]
    out_ref[3:6] = sum(x[0:3] for x in one_refs)
    at = 6
    for k in range(bias_refs[0].shape[0]):
        out_ref[at : at + 1] = bias_refs[0][k]
        at += 1
    for k in range(heads):
        row = pl.ds(index_ref[0] ^ k, 1)
        out_ref[at + k : at + k + 1, :wide] = sum(x[row] for x in heads_refs)


def small_sums(index, two, one, bias_up, heads, head_size):
    width = two.shape[1]
    count = 6 + bias_up[0].shape[0] + head_size
    inputs = [two, *one, *bias_up, *heads]
    return pl.pallas_call(
        functools.partial(small_sums_kernel, head_size),
        in_specs=[pl.BlockSpec(memory_space=pltpu.SMEM)]
        + [pl.BlockSpec(memory_space=pltpu.VMEM)] * len(inputs),
        out_specs=pl.BlockSpec(memory_space=pltpu.VMEM),
        out_shape=shape_of(f32, -(-count // 8) * 8, width),
        name="small_sums",
    )(index, *inputs)


def put_piece(piece, first, out_ref):
    half = piece.shape[0] // 2
    for n in range(2):
        at = pl.multiple_of((first ^ n) * half, half)
        out_ref[pl.ds(at, half)] = piece[n * half : (n + 1) * half].astype(f32)


def block_of(down):
    if down:
        return lambda i, index: (index[i], 0)
    return lambda i, index: (index[i] % 2, index[i] // 2)


def place_own_kernel(index_ref, *refs):
    out_ref, together_ref = refs[-2:]
    step = pl.program_id(0)
    for k, piece_ref in enumerate(refs[:-2]):

        @pl.when(step == k)
        def _():
            together_ref[0] = piece_ref[...]
            put_piece(piece_ref[...], index_ref[pl.num_programs(0) + step], out_ref)


def place_own(index, pieces, shape, down):
    count = len(pieces)
    rows, cols = pieces[0].shape
    return pl.pallas_call(
        place_own_kernel,
        grid_spec=pltpu.PrefetchScalarGridSpec(
            num_scalar_prefetch=1,
            grid=(count,),
            in_specs=[pl.BlockSpec((rows, cols), lambda i, index: (0, 0))] * count,
            out_specs=[
                pl.BlockSpec((rows, cols), block_of(down)),
                pl.BlockSpec((1, rows, cols), lambda i, index: (i, 0, 0)),
            ],
        ),
        out_shape=[shape_of(f32, *shape), shape_of(bf16, count, rows, cols)],
        compiler_params=params(16),
        cost_estimate=cost(0, 0),
        name="place_own",
    )(index, *pieces)


def place_other_kernel(index_ref, piece_ref, before_ref, out_ref):
    put_piece(piece_ref[0], index_ref[pl.num_programs(0) + pl.program_id(0)], out_ref)


def place_other(index, pieces, before, down):
    count, rows, cols = pieces.shape
    return pl.pallas_call(
        place_other_kernel,
        grid_spec=pltpu.PrefetchScalarGridSpec(
            num_scalar_prefetch=1,
            grid=(count,),
            in_specs=[
                pl.BlockSpec((1, rows, cols), lambda i, index: (i, 0, 0)),
                anywhere(),
            ],
            out_specs=pl.BlockSpec((rows, cols), block_of(down)),
        ),
        out_shape=shape_of(f32, *before.shape),
        input_output_aliases={2: 0},
        compiler_params=params(16),
        cost_estimate=cost(0, 0),
        name="place_other",
    )(index, pieces, before)


class Net:
    def __init__(self, dp_size, head_size):
        self.size = dp_size * head_size
        self.index = lax.axis_index("dp") * head_size + lax.axis_index("head")
        self.head_bits = [1 << k for k in range(head_size.bit_length() - 1)]
        self.dp_bits = [head_size << k for k in range(dp_size.bit_length() - 1)]
        self.core = self.head_bits[0]
        self.orders = [
            (self.dp_bits[0], self.head_bits[-1]),
            (self.head_bits[-1], self.dp_bits[0]),
        ]
        self.rest = self.head_bits[1:-1] + self.dp_bits[1:]

    def bit(self, mask):
        return (self.index // mask) % 2

    def swap(self, values, mask):
        return lax.ppermute(values, AXES, [(i, i ^ mask) for i in range(self.size)])


class Line:
    def __init__(self):
        self.last = ()

    def __call__(self, step, *inputs):
        inputs, _ = lax.optimization_barrier((inputs, self.last))
        result = step(*inputs)
        self.last = jax.tree.leaves(result)
        return result


def after(values, others):
    return lax.optimization_barrier((values, others))[0]


def half(values, which, axis):
    part = values.shape[axis] // 2
    return lax.dynamic_slice_in_dim(values, which * part, part, axis)


def plus(left, right):
    return (left.astype(f32) + right.astype(f32)).astype(bf16)


def join(own, mine, received, axis):
    return jnp.where(
        own == 0,
        jnp.concatenate([mine, received], axis),
        jnp.concatenate([received, mine], axis),
    )


def step_call(body, inputs, outputs, bits, name):
    return pl.pallas_call(
        body,
        in_specs=[pl.BlockSpec(memory_space=pltpu.SMEM)]
        + [pl.BlockSpec(memory_space=pltpu.VMEM)] * len(inputs),
        out_specs=[pl.BlockSpec(memory_space=pltpu.VMEM)] * len(outputs),
        out_shape=[shape_of(bf16, *x) for x in outputs],
        compiler_params=params(32),
        cost_estimate=cost(0, 0),
        name=name,
    )(jnp.stack(bits), *inputs)


def add_parts(kept, received):
    count, rows, cols = kept.shape

    def body(bits_ref, kept_ref, received_ref, *out_refs):
        for k in range(count):
            out_refs[k][...] = plus(kept_ref[k], received_ref[k])

    return step_call(body, [kept, received], [(rows, cols)] * count, [0], "add_parts")


def add_split(mine, received, axes, bits):
    count = len(mine)

    def halved(shape, axis):
        return shape[:axis] + (shape[axis] // 2,) + shape[axis + 1 :]

    def body(bits_ref, *refs):
        for k in range(count):
            mine_ref, received_ref, away_ref, keep_ref = refs[k::count]
            axis = axes[k]
            size = mine_ref.shape[axis] // 2
            for out_ref, which in ((away_ref, 1 - bits_ref[k]), (keep_ref, bits_ref[k])):
                here = (slice(None),) * axis + (pl.ds(which * size, size),)
                out_ref[...] = plus(mine_ref[here], received_ref[here])

    shapes = [halved(x.shape, axis) for x, axis in zip(mine, axes)]
    done = step_call(body, [*mine, *received], shapes * 2, bits, "add_split")
    return done[:count], done[count:]


def add_whole(mine, received):
    def body(bits_ref, mine_ref, received_ref, out_ref):
        out_ref[...] = plus(mine_ref[...], received_ref[...])

    return step_call(body, [mine, received], [mine.shape], [0], "add_whole")[0]


def join(mine, received, axis, bit):
    shape = mine.shape[:axis] + (2 * mine.shape[axis],) + mine.shape[axis + 1 :]

    def body(bits_ref, mine_ref, received_ref, out_ref):
        size = mine_ref.shape[axis]
        for ref, which in ((mine_ref, bits_ref[0]), (received_ref, 1 - bits_ref[0])):
            here = (slice(None),) * axis + (pl.ds(which * size, size),)
            out_ref[here] = ref[...]

    return step_call(body, [mine, received], [shape], [bit], "join")[0]


def travel(net, line, kept, received, shape, down, result):
    rows, cols = kept.shape[1:]
    small = 1 << len(net.rest)
    parts = line(add_parts, kept, received)
    received = [net.swap(away, order[0]) for away, order in zip(parts[1::2], net.orders)]
    yield

    def add_first(mine, received):
        mine, received = (
            [x.reshape(2 * small, rows // (2 * small), cols) for x in y] for y in (mine, received)
        )
        return add_split(mine, received, [0, 0], [net.bit(order[1]) for order in net.orders])

    away, mine = line(add_first, parts[0::2], received)
    received = [net.swap(x, order[1]) for x, order in zip(away, net.orders)]
    yield

    def add_second(mine, received):
        if not net.rest:
            return mine, [add_whole(x, y) for x, y in zip(mine, received)]
        return add_split(mine, received, [0, 0], [net.bit(net.rest[0])] * 2)

    away, mine = line(add_second, mine, received)
    for k, mask in enumerate(net.rest):
        away = away if k else jnp.stack(away)
        mine = mine if k else jnp.stack(mine)
        received = net.swap(away, mask)
        yield
        if k + 1 < len(net.rest):
            bit = net.bit(net.rest[k + 1])
            (away,), (mine,) = line(
                lambda x, y: add_split([x], [y], [1], [bit]), mine, received
            )
        else:
            mine = line(add_whole, mine, received)
    for mask in reversed(net.rest):
        received = net.swap(mine, mask)
        yield
        mine = line(lambda x, y: join(x, y, 1, net.bit(mask)), mine, received)
    mine = [mine[color] for color in (0, 1)]
    received = [net.swap(mine[color], order[1]) for color, order in enumerate(net.orders)]
    yield

    def join_second(mine, received):
        return [join(x, y, 0, 0 * net.bit(net.core)) for x, y in zip(mine, received)]

    near = [x.reshape(rows, cols) for x in line(join_second, mine, received)]
    far = [net.swap(x, order[0]) for x, order in zip(near, net.orders)]
    yield
    own, other = piece_index(net, 0), piece_index(net, 1)
    grad, pieces = line(
        functools.partial(place_own, shape=shape, down=down), own, near + far
    )
    received = net.swap(pieces, net.core)
    yield
    result.append(line(functools.partial(place_other, down=down), other, received, grad))


def travel_heads(net, line, kept, received, dp_size, finish, result):
    axis, *others = net.dp_bits
    last = net.head_bits[-1]
    own = net.bit(axis)
    for mask in net.head_bits[1:-1]:
        pairs = line(plus, kept, received)
        pairs = pairs.reshape((pairs.shape[0] // 2, 2) + pairs.shape[1:])
        kept, received = pairs[:, 0], net.swap(pairs[:, 1], mask)
        yield
    _, rows, cols = kept.shape
    each = rows // dp_size
    cut = cols // 2

    def add_core(kept, received):
        def body(bits_ref, kept_ref, received_ref, *out_refs):
            left = [plus(kept_ref[k, ..., :cut], received_ref[k, ..., :cut]) for k in (1, 0)]
            for out_ref, value in zip(out_refs, left):
                out_ref[...] = value
            for out_ref, which in zip(out_refs[2:], (1 - bits_ref[0], bits_ref[0])):
                for n in range(dp_size // 2):
                    here = (slice(None), 2 * n + which, slice(None), slice(cut, None))
                    out_ref[:, n] = plus(kept_ref[here], received_ref[here])

        kept, received = (x.reshape(2, dp_size, each, cols) for x in (kept, received))
        shapes = [(dp_size, each, cut)] * 2 + [(2, dp_size // 2, each, cut)] * 2
        return step_call(body, [kept, received], shapes, [own], "add_core")

    away_left, left, away_right, right = line(add_core, kept, received)
    received = [net.swap(away_left, last), net.swap(away_right, axis)]
    yield

    def add_first(left, right, received):
        def body(bits_ref, left_ref, right_ref, other_left_ref, other_right_ref, *out_refs):
            for out_ref, which in zip(out_refs, (1 - bits_ref[0], bits_ref[0])):
                for n in range(dp_size // 2):
                    out_ref[n] = plus(left_ref[2 * n + which], other_left_ref[2 * n + which])
            for out_ref, which in zip(out_refs[2:], (1, 0)):
                out_ref[...] = plus(right_ref[which], other_right_ref[which])

        shapes = [(dp_size // 2, each, cut)] * 4
        return step_call(body, [left, right, *received], shapes, [own], "add_first")

    away_left, left, away_right, right = line(add_first, left, right, received)
    received = [net.swap(away_left, axis), net.swap(away_right, last)]
    yield

    def add_second(left, right, received):
        def body(bits_ref, left_ref, right_ref, other_left_ref, other_right_ref, *out_refs):
            for out_ref, which in zip(out_refs, (1 - bits_ref[0], bits_ref[0])):
                size = out_ref.shape[0]
                here = pl.ds(which * size, size)
                out_ref[..., :cut] = plus(left_ref[here], other_left_ref[here])
                out_ref[..., cut:] = plus(right_ref[here], other_right_ref[here])

        shapes = [(dp_size // 4, each, cols)] * 2
        return step_call(
            body, [left, right, *received], shapes, [net.bit(others[-1])], "add_second"
        )

    away, mine = line(add_second, left, right, received)
    for k, mask in enumerate(reversed(others)):
        received = net.swap(away, mask)
        yield
        if k + 1 < len(others):
            bit = net.bit(others[-2 - k])
            (away,), (mine,) = line(
                lambda x, y: add_split([x], [y], [0], [bit]), mine, received
            )
    result.append(line(lambda x, y: finish(plus(x[0], y[0])), mine, received))


def add_sums(values, received):
    def body(values_ref, received_ref, out_ref):
        out_ref[...] = values_ref[...] + received_ref[...]

    return pl.pallas_call(
        body,
        out_shape=shape_of(f32, *values.shape),
        cost_estimate=cost(0, 0),
        name="add_sums",
    )(values, received)


def sum_everywhere(net, line, values, finish, result):
    for mask in net.head_bits + net.dp_bits:
        received = net.swap(values, mask)
        yield
        values = line(jnp.add, values, received)
    result.append(line(finish, values))


def piece_index(net, core):
    blocks, firsts = [], []
    for other in (0, 1):
        for color, (first, second) in enumerate(net.orders):
            square = 2 * (net.bit(net.core) ^ core) + color
            blocks.append(2 * square + (net.bit(first) ^ other))
            firsts.append(net.bit(second))
    return jnp.stack(blocks + firsts)


ORDER = "dBdUuAudHhusduhdsudhsudhsudhsududsu"


def shards(
    dp_size,
    head_size,
    tokens,
    cotangent,
    w_qkv,
    bias_qv,
    w_out,
    bias_out,
    gain_one,
    beta_one,
    w_up,
    bias_up,
    w_down,
    bias_down,
    gain_two,
    beta_two,
):
    net = Net(dp_size, head_size)
    model_width = tokens.shape[1]
    ff = w_up.shape[1]
    local_heads = w_qkv.shape[1]
    head_dim = w_qkv.shape[2] // 3
    wide = 3 * local_heads * head_dim
    scale = np.array([float(head_dim) ** -0.5, 1.0, 1.0], np.float32)
    bias = jnp.stack([bias_qv[:, 0], jnp.zeros_like(bias_qv[:, 0]), bias_qv[:, 1]], axis=1)
    scale_rows = jnp.asarray(np.repeat(np.tile(scale, local_heads), head_dim), bf16)
    payload = jnp.concatenate(
        [
            jnp.transpose(w_qkv, (1, 2, 0)).reshape(wide, model_width) * scale_rows[:, None],
            jnp.pad(
                (bias.reshape(wide) * scale_rows)[None], ((0, 15), (0, model_width - wide))
            ),
        ]
    )
    out_rows = w_out.reshape(-1, model_width)
    vectors = jnp.stack([bias_out, gain_one, beta_one, bias_down, gain_two, beta_two] + [bias_out] * 2)

    line = Line()
    attended, weights, out_weights = head_size, [], []
    for k in range(0, head_size, 2):
        own, own_out = payload, out_rows
        if k:
            own = after(net.swap(payload, k), attended)
            own_out = net.swap(after(out_rows, own), k)
        weights += [own, net.swap(own, net.core)]
        step = functools.partial(attend, heads=local_heads, place=k)
        if k:
            attended = line(step, tokens, weights[k:], attended)
            own_out = after(own_out, attended)
        else:
            attended = line(functools.partial(step, before=head_size), tokens, weights)
        out_weights += [own_out, net.swap(own_out, net.core)]
    projected, context, probs = attended
    core = net.bit(net.core)
    first_bits = [net.bit(order[0]) for order in net.orders]
    index = jnp.stack([2 * (1 - core), 3 - 2 * core, 2 * core, 2 * core + 1] + first_bits)
    down_pieces, up_pieces, attn_part, total = [], [], [], []
    slope, low, unit_one, scale_one, layer_out, grad_two, grad_ffn, sums_two, sent, kept = line(
        forward,
        index,
        tokens,
        cotangent,
        context,
        out_weights,
        w_up,
        w_down,
        vectors,
        bias_up.reshape(1, -1),
    )
    head_index = lax.axis_index("head")

    def finish_heads(rows):
        rows = rows.astype(f32)
        count = rows.shape[0]
        each = 3 * head_dim
        factor = jnp.asarray(np.repeat(scale, head_dim))
        grad_qkv = jnp.stack([rows[:, k * each : (k + 1) * each] * factor for k in range(local_heads)], 1)
        return grad_qkv, rows[:, wide:].T.reshape(local_heads, head_dim, count)

    def finish_sums(total):
        rows = ff // model_width
        parts = [total[k] for k in range(6)] + [total[6 : 6 + rows].reshape(-1)]
        own = lax.dynamic_index_in_dim(total[6 + rows :, :wide], head_index, 0, False)
        own = own.reshape(local_heads, 3, head_dim)
        pair = jnp.stack([own[:, 0] * scale[0], own[:, 2]], axis=1)
        cut = head_dim // dp_size
        return parts, lax.dynamic_slice_in_dim(pair, lax.axis_index("dp") * cut, cut, 2)

    tasks = {
        "d": travel(net, line, kept, net.swap(sent, net.core), w_down.shape, True, down_pieces)
    }
    for step in ORDER:
        if step == "B":
            grad_one, grad_att, sums_one, grad_bias_up, sent, kept = line(
                backward,
                index,
                grad_ffn,
                slope,
                grad_two,
                low,
                unit_one,
                scale_one,
                w_up,
                w_down,
                vectors,
            )
        elif step == "U":
            sent = net.swap(after(sent, line.last), net.core)
            tasks["u"] = travel(net, line, kept, sent, w_up.shape, False, up_pieces)
        elif step == "A":
            input_grad, sums_heads, sent, kept = line(
                functools.partial(attend_back, heads=local_heads),
                tokens,
                grad_att,
                grad_one,
                projected,
                probs,
                context,
                weights,
                out_weights,
            )
        elif step == "H":
            sent = net.swap(after(sent, line.last), net.core)
            tasks["h"] = travel_heads(net, line, kept, sent, dp_size, finish_heads, attn_part)
        elif step == "s" and "s" not in tasks:
            small = line(
                functools.partial(small_sums, head_size=head_size),
                head_index.reshape(1),
                sums_two,
                [sums_one],
                [grad_bias_up],
                [sums_heads],
            )
            tasks["s"] = sum_everywhere(net, line, small, finish_sums, total)
            next(tasks["s"])
        else:
            next(tasks[step], None)
    for task in tasks.values():
        for _ in task:
            pass
    grad_qkv, grad_out = attn_part[0]
    split, grad_bias_qv = total[0]
    full_down, full_up = down_pieces[0], up_pieces[0]
    return (
        layer_out,
        input_grad,
        grad_qkv,
        grad_bias_qv,
        grad_out,
        split[5],
        split[3],
        split[4],
        full_up,
        split[6],
        full_down,
        split[2],
        split[0],
        split[1],
    )


def solution(mesh):
    return jax.shard_map(
        functools.partial(shards, mesh.shape["dp"], mesh.shape["head"]),
        mesh=mesh,
        in_specs=(
            P(("dp", "head"), None),
            P(("dp", "head"), None),
            P(None, "head", None),
            P("head", None, None),
            P("head", None, None),
            P(),
            P(),
            P(),
            P(),
            P(),
            P(),
            P(),
            P(),
            P(),
        ),
        out_specs=(
            P(("dp", "head"), None),
            P(("dp", "head"), None),
            P("dp", "head", None),
            P("head", None, "dp"),
            P("head", None, "dp"),
            P(),
            P(),
            P(),
            P(),
            P(),
            P(),
            P(),
            P(),
            P(),
        ),
        check_vma=False,
    )
```

```python
import functools
import math

import jax
import jax.numpy as jnp
import numpy as np
from jax import lax
from jax.experimental import pallas as pl
from jax.experimental.pallas import tpu as pltpu
from jax.sharding import PartitionSpec as P

SEQ = 128
AXES = ("dp", "head")
f32 = jnp.float32
bf16 = jnp.bfloat16
epsilon = 1e-12
ROOM = 58

def dot(left, right, dims=(1, 0)):
    return lax.dot_general(
        left, right, (((dims[0],), (dims[1],)), ((), ())), preferred_element_type=f32
    )


def params(mib):
    return pltpu.CompilerParams(vmem_limit_bytes=mib * 1024 * 1024)


def cost(macs, moved, exps=0):
    return pl.CostEstimate(flops=1, bytes_accessed=1, transcendentals=0)


def whole(*shape):
    return pl.BlockSpec(shape, lambda *_: (0,) * len(shape))


def stay(*shape):
    return pl.BlockSpec(shape, lambda *_: (0,) * len(shape), pipeline_mode=pl.Buffered(1))


def anywhere():
    return pl.BlockSpec(memory_space=pl.ANY)


def shape_of(kind, *shape):
    return jax.ShapeDtypeStruct(shape, kind)


def column_sums(values):
    return jnp.sum(values, axis=0, keepdims=True)


def row_chunks(rows, heads, step=2 * SEQ):
    for begin in range(0, rows, step):
        yield [(at, head) for at in range(begin, begin + step, SEQ) for head in range(heads)]


def attend_kernel(heads, head_dim, parts, tokens_ref, *refs):
    weight_refs = refs[:parts]
    projected_ref, context_ref, probs_ref = refs[-3:]
    rows = tokens_ref.shape[0]
    wide = projected_ref.shape[2]
    for k, weight_ref in enumerate(weight_refs):

        @pl.when(pl.program_id(0) == k)
        def _():
            bias = weight_ref[wide : wide + 1, :wide].astype(f32)
            projected = dot(tokens_ref[...], weight_ref[:wide], (1, 1)) + bias
            projected_ref[0] = projected.astype(bf16)

    def part(start, head, which):
        at = (3 * head + which) * head_dim
        return projected_ref[0, start : start + SEQ, at : at + head_dim]

    for pairs in row_chunks(rows, heads):
        scores = [dot(part(s, h, 1), part(s, h, 0), (1, 1)) for s, h in pairs]
        exps = [jnp.exp(x - jnp.max(x, axis=0, keepdims=True)) for x in scores]
        probs = [(x * (1.0 / jnp.sum(x, axis=0, keepdims=True))).astype(bf16) for x in exps]
        for (s, h), p in zip(pairs, probs):
            probs_ref[h, s : s + SEQ] = p
        outs = [dot(p, part(s, h, 2), (0, 0)) for (s, h), p in zip(pairs, probs)]
        for k in range(0, len(pairs), heads):
            start = pairs[k][0]
            context_ref[0, start : start + SEQ] = jnp.concatenate(
                outs[k : k + heads], axis=1
            ).astype(bf16)


def attend(tokens, weights, before, heads, place):
    wide = weights[0].shape[0] - 16
    parts = len(weights)
    rows, width = tokens.shape
    head_dim = wide // (3 * heads)
    fresh = isinstance(before, int)
    groups = before if fresh else before[0].shape[0]
    before = [] if fresh else list(before)
    return pl.pallas_call(
        functools.partial(attend_kernel, heads, head_dim, parts),
        grid=(parts,),
        in_specs=[stay(rows, width)]
        + [stay(wide + 16, width)] * parts
        + [anywhere()] * len(before),
        out_specs=[
            pl.BlockSpec((1, rows, wide), lambda i: (i + place, 0, 0)),
            pl.BlockSpec((1, rows, wide // 3), lambda i: (i + place, 0, 0)),
            pl.BlockSpec((heads, rows, SEQ), lambda i: (i + place, 0, 0)),
        ],
        out_shape=[
            shape_of(bf16, groups, rows, wide),
            shape_of(bf16, groups, rows, wide // 3),
            shape_of(bf16, groups * heads, rows, SEQ),
        ],
        input_output_aliases={} if fresh else {1 + parts + k: k for k in range(3)},
        compiler_params=params(ROOM),
        cost_estimate=cost(parts * rows * wide * (width + 4 * SEQ), 4 * parts * rows * wide),
        name="attend",
    )(tokens, *weights, *before)


def normal(values):
    center = values - jnp.mean(values, axis=1, keepdims=True)
    inverse = lax.rsqrt(jnp.mean(center * center, axis=1, keepdims=True) + epsilon)
    return center * inverse, inverse


def normal_back(upstream, unit, inverse, gain):
    grad = upstream * gain
    return inverse * (
        grad
        - jnp.mean(grad, axis=1, keepdims=True)
        - unit * jnp.mean(grad * unit, axis=1, keepdims=True)
    )


def gelu_pair(values):
    spread = 0.5 + 0.5 * lax.erf(values * math.sqrt(0.5))
    density = jnp.exp2(values * values * (-0.5 * math.log2(math.e)))
    return values * spread, spread + values * (density * (1.0 / math.sqrt(2.0 * math.pi)))


def copies_between(pairs, semaphores):
    return [
        pltpu.make_async_copy(source, target, semaphores.at[k])
        for k, (source, target) in enumerate(pairs)
    ]


def half_squares(skip, half, width):
    return pl.BlockSpec((2, half, width), lambda i, *_: (jnp.clip(i - skip, 0, 1), 0, 0))


def forward_kernel(groups, tile, index_ref, tokens_ref, cot_hbm, context_ref, *refs):
    out_weight_refs, refs = refs[:groups], refs[groups:]
    w_up_ref, w_down_ref, vec_ref, bias_up_ref = refs[:4]
    slope_ref, low_hbm, unit_hbm, scale_hbm, out_hbm, grad_two_hbm, grad_ffn_hbm = refs[4:11]
    sums_ref, sent_ref, kept_ref = refs[11:14]
    low_ref, unit_ref, scale_ref, out_ref, grad_two_ref, grad_ffn_ref = refs[14:20]
    act_ref, total_ref, cot_ref, semaphores = refs[20:]
    step = pl.program_id(0)
    rows = tokens_ref.shape[0]
    vector = [vec_ref[k : k + 1] for k in range(6)]
    bias_out, gain_one, beta_one, bias_down, gain_two, beta_two = vector
    copies = copies_between(
        [
            (cot_hbm, cot_ref),
            (low_ref, low_hbm),
            (unit_ref, unit_hbm),
            (scale_ref, scale_hbm),
            (out_ref, out_hbm),
            (grad_two_ref, grad_two_hbm),
            (grad_ffn_ref, grad_ffn_hbm),
        ],
        semaphores,
    )

    @pl.when(step == 0)
    def _():
        copies[0].start()
        for start in range(0, rows, tile):
            here = slice(start, start + tile)
            attention = bias_out
            for group, weight_ref in enumerate(out_weight_refs):
                attention = attention + dot(context_ref[group, here], weight_ref[...])
            unit_one, scale_one = normal(tokens_ref[here].astype(f32) + attention)
            normed = unit_one * gain_one + beta_one
            unit_ref[here] = unit_one
            scale_ref[here] = scale_one
            low_ref[here] = normed.astype(bf16)
            total_ref[here] = normed + bias_down
        for copy in copies[1:4]:
            copy.start()

    @pl.when(step < 4)
    def _():
        cut = rows // 4
        parts = [slice(k * cut, (k + 1) * cut) for k in range(4)]
        hiddens = [dot(low_ref[here], w_up_ref[...]) + bias_up_ref[0] for here in parts]
        for here, hidden in zip(parts, hiddens):
            value, slope = gelu_pair(hidden)
            value = value.astype(bf16)
            act_ref[step, here] = value
            slope_ref[0, here] = slope.astype(bf16)
            total_ref[here] += dot(value, w_down_ref[...])

    @pl.when(step == 4)
    def _():
        copies[0].wait()
        sums = [0.0, 0.0, 0.0]
        for start in range(0, rows, tile):
            here = slice(start, start + tile)
            unit_two, scale_two = normal(total_ref[here])
            out_ref[here] = (unit_two * gain_two + beta_two).astype(bf16)
            upstream = cot_ref[here].astype(f32)
            grad_two = normal_back(upstream, unit_two, scale_two, gain_two)
            grad_two_ref[here] = grad_two
            grad_ffn = grad_two.astype(bf16)
            grad_ffn_ref[here] = grad_ffn
            terms = (upstream * unit_two, upstream, grad_ffn.astype(f32))
            sums = [x + column_sums(y) for x, y in zip(sums, terms)]
        for k in range(3):
            sums_ref[k : k + 1] = sums[k]
        for copy in copies[4:]:
            copy.start()

    for place, done_ref in enumerate((sent_ref, kept_ref)):

        @pl.when((step >= 4 + 2 * place) & (step < 6 + 2 * place))
        def _():
            square = index_ref[step - 4]
            first = index_ref[4 + step % 2]
            half = done_ref.shape[1]
            for n in range(2):
                left = act_ref[square, :, n * half : (n + 1) * half]
                done_ref[first ^ n] = dot(left, grad_ffn_ref[...], (0, 0)).astype(bf16)

    @pl.when(step == 7)
    def _():
        for copy in copies[1:]:
            copy.wait()


def forward(
    index, tokens, cotangent, context, out_weights, w_up, w_down, vectors, bias_up, tile=256
):
    rows, width = tokens.shape
    ff = w_up.shape[1]
    chunk = ff // 4
    kept = [(rows, width), (rows, width), (rows, 1)] + [(rows, width)] * 3
    kinds = [bf16, f32, f32, bf16, f32, bf16]
    return pl.pallas_call(
        functools.partial(forward_kernel, len(out_weights), tile),
        grid_spec=pltpu.PrefetchScalarGridSpec(
            num_scalar_prefetch=1,
            grid=(8,),
            in_specs=[stay(rows, width), anywhere(), stay(*context.shape)]
            + [stay(*w.shape) for w in out_weights]
            + [
                pl.BlockSpec((width, chunk), lambda i, *_: (0, jnp.minimum(i, 3))),
                pl.BlockSpec((chunk, width), lambda i, *_: (jnp.minimum(i, 3), 0)),
                stay(8, width),
                pl.BlockSpec((1, 1, chunk), lambda i, *_: (jnp.minimum(i, 3), 0, 0)),
            ],
            out_specs=[
                pl.BlockSpec((1, rows, chunk), lambda i, *_: (jnp.minimum(i, 3), 0, 0)),
                *([anywhere()] * 6),
                whole(8, width),
                half_squares(4, chunk // 2, width),
                half_squares(6, chunk // 2, width),
            ],
            scratch_shapes=[pltpu.VMEM(x, kind) for x, kind in zip(kept, kinds)]
            + [
                pltpu.VMEM((4, rows, chunk), bf16),
                pltpu.VMEM((rows, width), f32),
                pltpu.VMEM((rows, width), bf16),
                pltpu.SemaphoreType.DMA((7,)),
            ],
        ),
        out_shape=[shape_of(bf16, 4, rows, chunk)]
        + [shape_of(kind, *x) for x, kind in zip(kept, kinds)]
        + [
            shape_of(f32, 8, width),
            shape_of(bf16, 4, chunk // 2, width),
            shape_of(bf16, 4, chunk // 2, width),
        ],
        compiler_params=params(47),
        cost_estimate=cost(rows * width * (3 * ff + width), 12 * rows * ff, rows * ff),
        name="forward",
    )(
        index,
        tokens,
        cotangent,
        context,
        *out_weights,
        w_up,
        w_down,
        vectors,
        bias_up.reshape(4, 1, chunk),
    )


def backward_kernel(
    tile,
    index_ref,
    grad_ffn_ref,
    slope_ref,
    w_up_ref,
    w_down_ref,
    vec_ref,
    grad_two_hbm,
    low_hbm,
    unit_hbm,
    scale_hbm,
    grad_one_hbm,
    grad_att_hbm,
    sums_ref,
    bias_ref,
    sent_ref,
    kept_ref,
    total_ref,
    low_ref,
    unit_ref,
    scale_ref,
    grad_att_ref,
    grad_pre_ref,
    turned_ref,
    semaphores,
):
    step = pl.program_id(0)
    rows = grad_ffn_ref.shape[0]
    copies = copies_between(
        [
            (grad_two_hbm, total_ref),
            (low_hbm, low_ref),
            (unit_hbm, unit_ref),
            (scale_hbm, scale_ref),
            (total_ref, grad_one_hbm),
            (grad_att_ref, grad_att_hbm),
        ],
        semaphores,
    )

    @pl.when(step == 0)
    def _():
        for copy in copies[:4]:
            copy.start()

    @pl.when(step < 4)
    def _():
        grad_pre = dot(grad_ffn_ref[...], w_down_ref[...], (1, 1)) * slope_ref[0].astype(f32)
        grad_pre = grad_pre.astype(bf16)
        grad_pre_ref[step] = grad_pre
        bias_ref[0] = column_sums(grad_pre.astype(f32))

    @pl.when(step == 0)
    def _():
        for copy in copies[:2]:
            copy.wait()

    @pl.when(step < 4)
    def _():
        total_ref[...] += dot(grad_pre_ref[step], w_up_ref[...], (1, 1))

    @pl.when(step == 1)
    def _():
        turned_ref[...] = low_ref[...].T

    @pl.when(step == 4)
    def _():
        for copy in copies[2:4]:
            copy.wait()
        sums = [0.0, 0.0, 0.0]
        for start in range(0, rows, tile):
            here = slice(start, start + tile)
            total, unit = total_ref[here], unit_ref[here]
            grad_one = normal_back(total, unit, scale_ref[here], vec_ref[1:2])
            total_ref[here] = grad_one
            grad_att = grad_one.astype(bf16)
            grad_att_ref[here] = grad_att
            terms = (total * unit, total, grad_att.astype(f32))
            sums = [x + column_sums(y) for x, y in zip(sums, terms)]
        for k in range(3):
            sums_ref[k : k + 1] = sums[k]
        for copy in copies[4:]:
            copy.start()

    for place, done_ref in enumerate((sent_ref, kept_ref)):

        @pl.when((step >= 4 + 2 * place) & (step < 6 + 2 * place))
        def _():
            square = index_ref[step - 4]
            first = index_ref[4 + step % 2]
            half = done_ref.shape[1]
            for n in range(2):
                left = turned_ref[n * half : (n + 1) * half]
                done_ref[first ^ n] = dot(left, grad_pre_ref[square]).astype(bf16)

    @pl.when(step == 7)
    def _():
        for copy in copies[4:]:
            copy.wait()


def backward(
    index, grad_ffn, slope, grad_two, low, unit, scale, w_up, w_down, vectors, tile=256
):
    rows, width = grad_ffn.shape
    ff = w_up.shape[1]
    chunk = ff // 4
    return pl.pallas_call(
        functools.partial(backward_kernel, tile),
        grid_spec=pltpu.PrefetchScalarGridSpec(
            num_scalar_prefetch=1,
            grid=(8,),
            in_specs=[
                stay(rows, width),
                pl.BlockSpec((1, rows, chunk), lambda i, *_: (jnp.minimum(i, 3), 0, 0)),
                pl.BlockSpec((width, chunk), lambda i, *_: (0, jnp.minimum(i, 3))),
                pl.BlockSpec((chunk, width), lambda i, *_: (jnp.minimum(i, 3), 0)),
                stay(8, width),
                *([anywhere()] * 4),
            ],
            out_specs=[
                anywhere(),
                anywhere(),
                whole(8, width),
                pl.BlockSpec((1, 1, chunk), lambda i, *_: (jnp.minimum(i, 3), 0, 0)),
                half_squares(4, width // 2, chunk),
                half_squares(6, width // 2, chunk),
            ],
            scratch_shapes=[
                pltpu.VMEM((rows, width), f32),
                pltpu.VMEM((rows, width), bf16),
                pltpu.VMEM((rows, width), f32),
                pltpu.VMEM((rows, 1), f32),
                pltpu.VMEM((rows, width), bf16),
                pltpu.VMEM((4, rows, chunk), bf16),
                pltpu.VMEM((width, rows), bf16),
                pltpu.SemaphoreType.DMA((6,)),
            ],
        ),
        out_shape=[
            shape_of(f32, rows, width),
            shape_of(bf16, rows, width),
            shape_of(f32, 8, width),
            shape_of(f32, 4, 1, chunk),
            shape_of(bf16, 4, width // 2, chunk),
            shape_of(bf16, 4, width // 2, chunk),
        ],
        compiler_params=params(ROOM),
        cost_estimate=cost(rows * width * 3 * ff, 10 * rows * ff),
        name="backward",
    )(index, grad_ffn, slope, w_up, w_down, vectors, grad_two, low, unit, scale)


def attend_back_kernel(
    heads,
    head_dim,
    groups,
    tokens_ref,
    grad_att_ref,
    grad_one_hbm,
    projected_ref,
    probs_ref,
    context_ref,
    *refs,
):
    weight_refs, refs = refs[:groups], refs[groups:]
    out_weight_refs, refs = refs[:groups], refs[groups:]
    input_hbm, sums_ref, sent_ref, kept_ref = refs[:4]
    grad_projected_ref, grad_context_ref, total_ref, tokens_t, grad_att_t, semaphores = refs[4:]
    step = pl.program_id(0)
    rows, wide = grad_projected_ref.shape
    order = list(range(1, groups, 2)) + list(range(0, groups, 2))
    copies = copies_between([(grad_one_hbm, total_ref), (total_ref, input_hbm)], semaphores)

    @pl.when(step == 0)
    def _():
        copies[0].start()
        sums_ref[...] = jnp.zeros_like(sums_ref)
        tokens_t[...] = tokens_ref[...].T
        grad_att_t[...] = grad_att_ref[...].T

    for k, group in enumerate(order):

        @pl.when(step == k)
        def _():
            grad_context_ref[...] = dot(
                grad_att_ref[...], out_weight_refs[group][...], (1, 1)
            ).astype(bf16)

    def part(start, head, which):
        at = (3 * head + which) * head_dim
        return projected_ref[0, start : start + SEQ, at : at + head_dim]

    def up(start, head):
        return grad_context_ref[start : start + SEQ, head * head_dim : (head + 1) * head_dim]

    def low(start, head):
        return probs_ref[head, start : start + SEQ]

    for pairs in row_chunks(rows, heads):
        grad_probs = [dot(part(s, h, 2), up(s, h), (1, 1)) for s, h in pairs]
        probs = [low(s, h).astype(f32) for s, h in pairs]
        inner = [jnp.sum(x * p, axis=0, keepdims=True) for x, p in zip(grad_probs, probs)]
        grad_scores = [(p * (x - i)).astype(bf16) for x, i, p in zip(grad_probs, inner, probs)]
        grad_v = [dot(low(s, h), up(s, h)) for s, h in pairs]
        grad_k = [dot(x, part(s, h, 0)) for x, (s, h) in zip(grad_scores, pairs)]
        grad_q = [dot(x, part(s, h, 1), (0, 0)) for x, (s, h) in zip(grad_scores, pairs)]
        for k in range(0, len(pairs), heads):
            start = pairs[k][0]
            pieces = [x for j in range(k, k + heads) for x in (grad_q[j], grad_k[j], grad_v[j])]
            grad_projected_ref[start : start + SEQ] = jnp.concatenate(pieces, axis=1).astype(bf16)

    @pl.when(step == 0)
    def _():
        copies[0].wait()

    for k, group in enumerate(order):

        @pl.when(step == k)
        def _():
            grad_projected = grad_projected_ref[...]
            sums_ref[group : group + 1] = column_sums(grad_projected.astype(f32))
            total_ref[...] += dot(grad_projected, weight_refs[group][:wide])

    @pl.when(step == groups - 1)
    def _():
        copies[1].start()

    for place, done_ref in enumerate((sent_ref, kept_ref)):

        @pl.when(step // (groups // 2) == place)
        def _():
            done_ref[0, :, :wide] = dot(tokens_t[...], grad_projected_ref[...]).astype(bf16)
            done_ref[0, :, wide:] = dot(grad_att_t[...], context_ref[0]).astype(bf16)

    @pl.when(step == groups - 1)
    def _():
        copies[1].wait()


def attend_back(
    tokens, grad_att, grad_one, projected, probs, context, weights, out_weights, heads
):
    wide = weights[0].shape[0] - 16
    deep = context.shape[2]
    rows, width = grad_att.shape
    head_dim = wide // (3 * heads)
    groups = len(weights)
    pairs = groups // 2

    def group(i):
        return jnp.where(i < pairs, 2 * i + 1, 2 * (i - pairs))

    def by_group(count, columns):
        return pl.BlockSpec((count, rows, columns), lambda i: (group(i), 0, 0))

    def done(skip):
        return pl.BlockSpec(
            (1, width, wide + deep), lambda i: (jnp.clip(i - skip, 0, pairs - 1), 0, 0)
        )

    return pl.pallas_call(
        functools.partial(attend_back_kernel, heads, head_dim, groups),
        grid=(groups,),
        in_specs=[
            stay(rows, width),
            stay(rows, width),
            anywhere(),
            by_group(1, wide),
            by_group(heads, SEQ),
            by_group(1, deep),
        ]
        + [stay(*x.shape) for x in weights]
        + [stay(*x.shape) for x in out_weights],
        out_specs=[anywhere(), whole(8, wide), done(0), done(pairs)],
        out_shape=[
            shape_of(f32, rows, width),
            shape_of(f32, 8, wide),
            shape_of(bf16, pairs, width, wide + deep),
            shape_of(bf16, pairs, width, wide + deep),
        ],
        scratch_shapes=[
            pltpu.VMEM((rows, wide), bf16),
            pltpu.VMEM((rows, deep), bf16),
            pltpu.VMEM((rows, width), f32),
            pltpu.VMEM((width, rows), bf16),
            pltpu.VMEM((width, rows), bf16),
            pltpu.SemaphoreType.DMA((2,)),
        ],
        compiler_params=params(ROOM),
        cost_estimate=cost(groups * rows * wide * (width * 4 // 3 + 10 * SEQ), 8 * groups * rows * wide),
        name="attend_back",
    )(tokens, grad_att, grad_one, projected, probs, context, *weights, *out_weights)


def small_sums_kernel(heads, index_ref, two_ref, *refs):
    out_ref = refs[-1]
    out_ref[...] = jnp.zeros_like(out_ref)
    one_refs, bias_refs, heads_refs = refs[:1], refs[1:2], refs[2:-1]
    width = out_ref.shape[1]
    wide = heads_refs[0].shape[1]
    out_ref[0:3] = two_ref[0:3]
    out_ref[3:6] = sum(x[0:3] for x in one_refs)
    at = 6
    for k in range(bias_refs[0].shape[0]):
        out_ref[at : at + 1] = bias_refs[0][k]
        at += 1
    for k in range(heads):
        row = pl.ds(index_ref[0] ^ k, 1)
        out_ref[at + k : at + k + 1, :wide] = sum(x[row] for x in heads_refs)


def small_sums(index, two, one, bias_up, heads, head_size):
    width = two.shape[1]
    count = 6 + bias_up[0].shape[0] + head_size
    inputs = [two, *one, *bias_up, *heads]
    return pl.pallas_call(
        functools.partial(small_sums_kernel, head_size),
        in_specs=[pl.BlockSpec(memory_space=pltpu.SMEM)]
        + [pl.BlockSpec(memory_space=pltpu.VMEM)] * len(inputs),
        out_specs=pl.BlockSpec(memory_space=pltpu.VMEM),
        out_shape=shape_of(f32, -(-count // 8) * 8, width),
        name="small_sums",
    )(index, *inputs)


def put_piece(piece, first, out_ref):
    half = piece.shape[0] // 2
    for n in range(2):
        at = pl.multiple_of((first ^ n) * half, half)
        out_ref[pl.ds(at, half)] = piece[n * half : (n + 1) * half].astype(f32)


def block_of(down):
    if down:
        return lambda i, index: (index[i], 0)
    return lambda i, index: (index[i] % 2, index[i] // 2)


def place_own_kernel(index_ref, *refs):
    out_ref, together_ref = refs[-2:]
    step = pl.program_id(0)
    for k, piece_ref in enumerate(refs[:-2]):

        @pl.when(step == k)
        def _():
            together_ref[0] = piece_ref[...]
            put_piece(piece_ref[...], index_ref[pl.num_programs(0) + step], out_ref)


def place_own(index, pieces, shape, down):
    count = len(pieces)
    rows, cols = pieces[0].shape
    return pl.pallas_call(
        place_own_kernel,
        grid_spec=pltpu.PrefetchScalarGridSpec(
            num_scalar_prefetch=1,
            grid=(count,),
            in_specs=[pl.BlockSpec((rows, cols), lambda i, index: (0, 0))] * count,
            out_specs=[
                pl.BlockSpec((rows, cols), block_of(down)),
                pl.BlockSpec((1, rows, cols), lambda i, index: (i, 0, 0)),
            ],
        ),
        out_shape=[shape_of(f32, *shape), shape_of(bf16, count, rows, cols)],
        compiler_params=params(16),
        cost_estimate=cost(0, 0),
        name="place_own",
    )(index, *pieces)


def place_other_kernel(index_ref, piece_ref, before_ref, out_ref):
    put_piece(piece_ref[0], index_ref[pl.num_programs(0) + pl.program_id(0)], out_ref)


def place_other(index, pieces, before, down):
    count, rows, cols = pieces.shape
    return pl.pallas_call(
        place_other_kernel,
        grid_spec=pltpu.PrefetchScalarGridSpec(
            num_scalar_prefetch=1,
            grid=(count,),
            in_specs=[
                pl.BlockSpec((1, rows, cols), lambda i, index: (i, 0, 0)),
                anywhere(),
            ],
            out_specs=pl.BlockSpec((rows, cols), block_of(down)),
        ),
        out_shape=shape_of(f32, *before.shape),
        input_output_aliases={2: 0},
        compiler_params=params(16),
        cost_estimate=cost(0, 0),
        name="place_other",
    )(index, pieces, before)


class Net:
    def __init__(self, dp_size, head_size):
        self.size = dp_size * head_size
        self.index = lax.axis_index("dp") * head_size + lax.axis_index("head")
        self.head_bits = [1 << k for k in range(head_size.bit_length() - 1)]
        self.dp_bits = [head_size << k for k in range(dp_size.bit_length() - 1)]
        self.core = self.head_bits[0]
        self.orders = [
            (self.dp_bits[0], self.head_bits[-1]),
            (self.head_bits[-1], self.dp_bits[0]),
        ]
        self.rest = self.head_bits[1:-1] + self.dp_bits[1:]

    def bit(self, mask):
        return (self.index // mask) % 2

    def swap(self, values, mask):
        return lax.ppermute(values, AXES, [(i, i ^ mask) for i in range(self.size)])


class Line:
    def __init__(self):
        self.last = ()

    def __call__(self, step, *inputs):
        inputs, _ = lax.optimization_barrier((inputs, self.last))
        result = step(*inputs)
        self.last = jax.tree.leaves(result)
        return result


def after(values, others):
    return lax.optimization_barrier((values, others))[0]


def half(values, which, axis):
    part = values.shape[axis] // 2
    return lax.dynamic_slice_in_dim(values, which * part, part, axis)


def plus(left, right):
    return (left.astype(f32) + right.astype(f32)).astype(bf16)


def join(own, mine, received, axis):
    return jnp.where(
        own == 0,
        jnp.concatenate([mine, received], axis),
        jnp.concatenate([received, mine], axis),
    )


def step_call(body, inputs, outputs, bits, name):
    return pl.pallas_call(
        body,
        in_specs=[pl.BlockSpec(memory_space=pltpu.SMEM)]
        + [pl.BlockSpec(memory_space=pltpu.VMEM)] * len(inputs),
        out_specs=[pl.BlockSpec(memory_space=pltpu.VMEM)] * len(outputs),
        out_shape=[shape_of(bf16, *x) for x in outputs],
        compiler_params=params(32),
        cost_estimate=cost(0, 0),
        name=name,
    )(jnp.stack(bits), *inputs)


def add_parts(kept, received):
    count, rows, cols = kept.shape

    def body(bits_ref, kept_ref, received_ref, *out_refs):
        for k in range(count):
            out_refs[k][...] = plus(kept_ref[k], received_ref[k])

    return step_call(body, [kept, received], [(rows, cols)] * count, [0], "add_parts")


def add_split(mine, received, axes, bits):
    count = len(mine)

    def halved(shape, axis):
        return shape[:axis] + (shape[axis] // 2,) + shape[axis + 1 :]

    def body(bits_ref, *refs):
        for k in range(count):
            mine_ref, received_ref, away_ref, keep_ref = refs[k::count]
            axis = axes[k]
            size = mine_ref.shape[axis] // 2
            for out_ref, which in ((away_ref, 1 - bits_ref[k]), (keep_ref, bits_ref[k])):
                here = (slice(None),) * axis + (pl.ds(which * size, size),)
                out_ref[...] = plus(mine_ref[here], received_ref[here])

    shapes = [halved(x.shape, axis) for x, axis in zip(mine, axes)]
    done = step_call(body, [*mine, *received], shapes * 2, bits, "add_split")
    return done[:count], done[count:]


def add_whole(mine, received):
    def body(bits_ref, mine_ref, received_ref, out_ref):
        out_ref[...] = plus(mine_ref[...], received_ref[...])

    return step_call(body, [mine, received], [mine.shape], [0], "add_whole")[0]


def join(mine, received, axis, bit):
    shape = mine.shape[:axis] + (2 * mine.shape[axis],) + mine.shape[axis + 1 :]

    def body(bits_ref, mine_ref, received_ref, out_ref):
        size = mine_ref.shape[axis]
        for ref, which in ((mine_ref, bits_ref[0]), (received_ref, 1 - bits_ref[0])):
            here = (slice(None),) * axis + (pl.ds(which * size, size),)
            out_ref[here] = ref[...]

    return step_call(body, [mine, received], [shape], [bit], "join")[0]


def travel(net, line, kept, received, shape, down, result):
    rows, cols = kept.shape[1:]
    small = 1 << len(net.rest)
    parts = line(add_parts, kept, received)
    received = [net.swap(away, order[0]) for away, order in zip(parts[1::2], net.orders)]
    yield

    def add_first(mine, received):
        mine, received = (
            [x.reshape(2 * small, rows // (2 * small), cols) for x in y] for y in (mine, received)
        )
        return add_split(mine, received, [0, 0], [net.bit(order[1]) for order in net.orders])

    away, mine = line(add_first, parts[0::2], received)
    received = [net.swap(x, order[1]) for x, order in zip(away, net.orders)]
    yield

    def add_second(mine, received):
        if not net.rest:
            return mine, [add_whole(x, y) for x, y in zip(mine, received)]
        return add_split(mine, received, [0, 0], [net.bit(net.rest[0])] * 2)

    away, mine = line(add_second, mine, received)
    for k, mask in enumerate(net.rest):
        away = away if k else jnp.stack(away)
        mine = mine if k else jnp.stack(mine)
        received = net.swap(away, mask)
        yield
        if k + 1 < len(net.rest):
            bit = net.bit(net.rest[k + 1])
            (away,), (mine,) = line(
                lambda x, y: add_split([x], [y], [1], [bit]), mine, received
            )
        else:
            mine = line(add_whole, mine, received)
    for mask in reversed(net.rest):
        received = net.swap(mine, mask)
        yield
        mine = line(lambda x, y: join(x, y, 1, net.bit(mask)), mine, received)
    mine = [mine[color] for color in (0, 1)]
    received = [net.swap(mine[color], order[1]) for color, order in enumerate(net.orders)]
    yield

    def join_second(mine, received):
        return [join(x, y, 0, 0 * net.bit(net.core)) for x, y in zip(mine, received)]

    near = [x.reshape(rows, cols) for x in line(join_second, mine, received)]
    far = [net.swap(x, order[0]) for x, order in zip(near, net.orders)]
    yield
    own, other = piece_index(net, 0), piece_index(net, 1)
    grad, pieces = line(
        functools.partial(place_own, shape=shape, down=down), own, near + far
    )
    received = net.swap(pieces, net.core)
    yield
    result.append(line(functools.partial(place_other, down=down), other, received, grad))


def travel_heads(net, line, kept, received, dp_size, finish, result):
    axis, *others = net.dp_bits
    last = net.head_bits[-1]
    own = net.bit(axis)
    for mask in net.head_bits[1:-1]:
        pairs = line(plus, kept, received)
        pairs = pairs.reshape((pairs.shape[0] // 2, 2) + pairs.shape[1:])
        kept, received = pairs[:, 0], net.swap(pairs[:, 1], mask)
        yield
    _, rows, cols = kept.shape
    each = rows // dp_size
    cut = cols // 2

    def add_core(kept, received):
        def body(bits_ref, kept_ref, received_ref, *out_refs):
            left = [plus(kept_ref[k, ..., :cut], received_ref[k, ..., :cut]) for k in (1, 0)]
            for out_ref, value in zip(out_refs, left):
                out_ref[...] = value
            for out_ref, which in zip(out_refs[2:], (1 - bits_ref[0], bits_ref[0])):
                for n in range(dp_size // 2):
                    here = (slice(None), 2 * n + which, slice(None), slice(cut, None))
                    out_ref[:, n] = plus(kept_ref[here], received_ref[here])

        kept, received = (x.reshape(2, dp_size, each, cols) for x in (kept, received))
        shapes = [(dp_size, each, cut)] * 2 + [(2, dp_size // 2, each, cut)] * 2
        return step_call(body, [kept, received], shapes, [own], "add_core")

    away_left, left, away_right, right = line(add_core, kept, received)
    received = [net.swap(away_left, last), net.swap(away_right, axis)]
    yield

    def add_first(left, right, received):
        def body(bits_ref, left_ref, right_ref, other_left_ref, other_right_ref, *out_refs):
            for out_ref, which in zip(out_refs, (1 - bits_ref[0], bits_ref[0])):
                for n in range(dp_size // 2):
                    out_ref[n] = plus(left_ref[2 * n + which], other_left_ref[2 * n + which])
            for out_ref, which in zip(out_refs[2:], (1, 0)):
                out_ref[...] = plus(right_ref[which], other_right_ref[which])

        shapes = [(dp_size // 2, each, cut)] * 4
        return step_call(body, [left, right, *received], shapes, [own], "add_first")

    away_left, left, away_right, right = line(add_first, left, right, received)
    received = [net.swap(away_left, axis), net.swap(away_right, last)]
    yield

    def add_second(left, right, received):
        def body(bits_ref, left_ref, right_ref, other_left_ref, other_right_ref, *out_refs):
            for out_ref, which in zip(out_refs, (1 - bits_ref[0], bits_ref[0])):
                size = out_ref.shape[0]
                here = pl.ds(which * size, size)
                out_ref[..., :cut] = plus(left_ref[here], other_left_ref[here])
                out_ref[..., cut:] = plus(right_ref[here], other_right_ref[here])

        shapes = [(dp_size // 4, each, cols)] * 2
        return step_call(
            body, [left, right, *received], shapes, [net.bit(others[-1])], "add_second"
        )

    away, mine = line(add_second, left, right, received)
    for k, mask in enumerate(reversed(others)):
        received = net.swap(away, mask)
        yield
        if k + 1 < len(others):
            bit = net.bit(others[-2 - k])
            (away,), (mine,) = line(
                lambda x, y: add_split([x], [y], [0], [bit]), mine, received
            )
    result.append(line(lambda x, y: finish(plus(x[0], y[0])), mine, received))


def add_sums(values, received):
    def body(values_ref, received_ref, out_ref):
        out_ref[...] = values_ref[...] + received_ref[...]

    return pl.pallas_call(
        body,
        out_shape=shape_of(f32, *values.shape),
        cost_estimate=cost(0, 0),
        name="add_sums",
    )(values, received)


def sum_everywhere(net, line, values, finish, result):
    for mask in net.head_bits + net.dp_bits:
        received = net.swap(values, mask)
        yield
        values = line(jnp.add, values, received)
    result.append(line(finish, values))


def piece_index(net, core):
    blocks, firsts = [], []
    for other in (0, 1):
        for color, (first, second) in enumerate(net.orders):
            square = 2 * (net.bit(net.core) ^ core) + color
            blocks.append(2 * square + (net.bit(first) ^ other))
            firsts.append(net.bit(second))
    return jnp.stack(blocks + firsts)


ORDER = "dBdUuAudHhusduhdsudhsudhsudhsududsu"


def shards(
    dp_size,
    head_size,
    tokens,
    cotangent,
    w_qkv,
    bias_qv,
    w_out,
    bias_out,
    gain_one,
    beta_one,
    w_up,
    bias_up,
    w_down,
    bias_down,
    gain_two,
    beta_two,
):
    net = Net(dp_size, head_size)
    model_width = tokens.shape[1]
    ff = w_up.shape[1]
    local_heads = w_qkv.shape[1]
    head_dim = w_qkv.shape[2] // 3
    wide = 3 * local_heads * head_dim
    scale = np.array([float(head_dim) ** -0.5, 1.0, 1.0], np.float32)
    bias = jnp.concatenate(
        [
            bias_qv[:, :1] * jnp.asarray(scale[0], bf16),
            jnp.zeros_like(bias_qv[:, :1]),
            bias_qv[:, 1:],
        ],
        axis=1,
    )
    scale_rows = jnp.asarray(np.repeat(np.tile(scale, local_heads), head_dim), bf16)
    payload = jnp.concatenate(
        [
            jnp.transpose(w_qkv, (1, 2, 0)).reshape(wide, model_width) * scale_rows[:, None],
            jnp.pad(
                bias.reshape(1, wide), ((0, 15), (0, model_width - wide))
            ),
        ]
    )
    out_rows = w_out.reshape(-1, model_width)
    vectors = jnp.stack([bias_out, gain_one, beta_one, bias_down, gain_two, beta_two] + [bias_out] * 2)

    line = Line()
    attended, weights, out_weights = head_size, [], []
    for k in range(0, head_size, 2):
        own, own_out = payload, out_rows
        if k:
            own = after(net.swap(payload, k), attended)
            own_out = net.swap(after(out_rows, own), k)
        weights += [own, net.swap(own, net.core)]
        step = functools.partial(attend, heads=local_heads, place=k)
        if k:
            attended = line(step, tokens, weights[k:], attended)
            own_out = after(own_out, attended)
        else:
            attended = line(functools.partial(step, before=head_size), tokens, weights)
        out_weights += [own_out, net.swap(own_out, net.core)]
    projected, context, probs = attended
    core = net.bit(net.core)
    first_bits = [net.bit(order[0]) for order in net.orders]
    index = jnp.stack([2 * (1 - core), 3 - 2 * core, 2 * core, 2 * core + 1] + first_bits)
    down_pieces, up_pieces, attn_part, total = [], [], [], []
    slope, low, unit_one, scale_one, layer_out, grad_two, grad_ffn, sums_two, sent, kept = line(
        forward,
        index,
        tokens,
        cotangent,
        context,
        out_weights,
        w_up,
        w_down,
        vectors,
        bias_up.reshape(1, -1),
    )
    head_index = lax.axis_index("head")

    def finish_heads(rows):
        rows = rows.astype(f32)
        count = rows.shape[0]
        each = 3 * head_dim
        factor = jnp.asarray(np.repeat(scale, head_dim))
        grad_qkv = jnp.stack([rows[:, k * each : (k + 1) * each] * factor for k in range(local_heads)], 1)
        return grad_qkv, rows[:, wide:].T.reshape(local_heads, head_dim, count)

    def finish_sums(total):
        rows = ff // model_width
        parts = [total[k] for k in range(6)] + [total[6 : 6 + rows].reshape(-1)]
        own = lax.dynamic_index_in_dim(total[6 + rows :, :wide], head_index, 0, False)
        own = own.reshape(local_heads, 3, head_dim)
        pair = jnp.stack([own[:, 0] * scale[0], own[:, 2]], axis=1)
        cut = head_dim // dp_size
        return parts, lax.dynamic_slice_in_dim(pair, lax.axis_index("dp") * cut, cut, 2)

    tasks = {
        "d": travel(net, line, kept, net.swap(sent, net.core), w_down.shape, True, down_pieces)
    }
    for step in ORDER:
        if step == "B":
            grad_one, grad_att, sums_one, grad_bias_up, sent, kept = line(
                backward,
                index,
                grad_ffn,
                slope,
                grad_two,
                low,
                unit_one,
                scale_one,
                w_up,
                w_down,
                vectors,
            )
        elif step == "U":
            sent = net.swap(after(sent, line.last), net.core)
            tasks["u"] = travel(net, line, kept, sent, w_up.shape, False, up_pieces)
        elif step == "A":
            input_grad, sums_heads, sent, kept = line(
                functools.partial(attend_back, heads=local_heads),
                tokens,
                grad_att,
                grad_one,
                projected,
                probs,
                context,
                weights,
                out_weights,
            )
        elif step == "H":
            sent = net.swap(after(sent, line.last), net.core)
            tasks["h"] = travel_heads(net, line, kept, sent, dp_size, finish_heads, attn_part)
        elif step == "s" and "s" not in tasks:
            small = line(
                functools.partial(small_sums, head_size=head_size),
                head_index.reshape(1),
                sums_two,
                [sums_one],
                [grad_bias_up],
                [sums_heads],
            )
            tasks["s"] = sum_everywhere(net, line, small, finish_sums, total)
            next(tasks["s"])
        else:
            next(tasks[step], None)
    for task in tasks.values():
        for _ in task:
            pass
    grad_qkv, grad_out = attn_part[0]
    split, grad_bias_qv = total[0]
    full_down, full_up = down_pieces[0], up_pieces[0]
    return (
        layer_out,
        input_grad,
        grad_qkv,
        grad_bias_qv,
        grad_out,
        split[5],
        split[3],
        split[4],
        full_up,
        split[6],
        full_down,
        split[2],
        split[0],
        split[1],
    )


def solution(mesh):
    return jax.shard_map(
        functools.partial(shards, mesh.shape["dp"], mesh.shape["head"]),
        mesh=mesh,
        in_specs=(
            P(("dp", "head"), None),
            P(("dp", "head"), None),
            P(None, "head", None),
            P("head", None, None),
            P("head", None, None),
            P(),
            P(),
            P(),
            P(),
            P(),
            P(),
            P(),
            P(),
            P(),
        ),
        out_specs=(
            P(("dp", "head"), None),
            P(("dp", "head"), None),
            P("dp", "head", None),
            P("head", None, "dp"),
            P("head", None, "dp"),
            P(),
            P(),
            P(),
            P(),
            P(),
            P(),
            P(),
            P(),
            P(),
        ),
        check_vma=False,
    )
```
